512 devices in a mesh: row: 16 (over y, x), col: 32 (over z, core).
Axes of the slice: x: 4, y: 4, z: 16, core: 2. Of those that a mesh axis runs over, the one named last changes fastest.
Arguments:
- three_centre: bfloat16 [256, 1024, 1024], P('col', 'row'), may hold values from -6 to 6
- density: bfloat16 [1024, 1024], P('col'), may hold values from -0.00036621094 to 0.00036621094
- pair_mask: int32 [16, 16], replicated, may hold values 0 or 1
- density_mask: int32 [16, 16], replicated, may hold values 0 or 1
Outputs:
- exchange_matrix: float32 [1024, 1024], P('row', 'col')
The draws below stay inside these ranges and needn't reach their ends.
All inputs are finite; a program needn't handle non-finite values.
Results may differ from the reference program's by a relative error of at most 0.0029.
Values may be sent and summed in bfloat16 or wider, within the bound.
No kernel may reach another device: no remote copies, remote signals or barrier semaphores. Data moves between devices by JAX's collectives and lax.ppermute only.
A program may use at most 64 MiB of HBM per device.

```python
import jax
import jax.numpy as jnp
from jax import lax

BLK = 64
NBLK = 16
BASIS = 1024
AUX = 256


def touch_ends(result, rng, least, high):
    extent = result.shape
    spot = [jax.random.randint(jax.random.fold_in(rng, axis), (), 0, extent[axis]) for axis in range(len(extent))]
    result = result.at[tuple(spot)].set(least)
    longest = extent.index(max(extent))
    spot[longest] = (spot[longest] + 1) % extent[longest]
    return result.at[tuple(spot)].set(high)


def raised(drawn, own_key, source, target, parts, factor):
    def block_of(position):
        return (jnp.arange(drawn.shape[position]) // (drawn.shape[position] // parts)).reshape((-1,) + (1,) * (drawn.ndim - 1 - position))

    first = jax.random.permutation(own_key, parts)[block_of(target)]
    second = (block_of(target) + parts // 2) % parts
    return jnp.where((block_of(source) == first) | (block_of(source) == second), factor * drawn, drawn)


def block_levels(stream_key, shape, split, least, top_value):
    gain, own = 1.0, jax.random.fold_in(stream_key, 6)
    for dim, blocks in split:
        draws = jnp.exp(jax.random.uniform(jax.random.fold_in(own, dim), (blocks,), jnp.float32, least / len(split), top_value / len(split)))
        gain = gain * jnp.repeat(draws, shape[dim] // blocks).reshape([-1 if axis == dim else 1 for axis in range(len(shape))])
    return gain


def normal_values(rng, dims, width, most, pieces=(), kind=jnp.bfloat16):
    array = jax.random.normal(rng, dims, jnp.float32) * width
    if len(pieces) > 0:
        array = block_levels(rng, dims, pieces, -0.22, 0.18) * array
    return jnp.clip(array, min=-most, max=most).astype(kind)


def heavy_noise(stream_key, dims, scale, limit, shards, heavy, kind=jnp.bfloat16):
    drawn = scale * jax.random.normal(stream_key, dims, jnp.float32)
    if shards:
        drawn = drawn * block_levels(stream_key, dims, shards, -0.22, 0.18)
    return jnp.clip(raised(drawn, jax.random.fold_in(stream_key, 3), *heavy), -limit, limit).astype(kind)


def setup_inputs(seed: int = 0) -> dict:
    key_list = jax.random.split(jax.random.key(seed), 5)
    three_centre = heavy_noise(key_list[0], (AUX, BASIS, BASIS), 1.0, 6.0, ((0, 32), (1, 16)), (0, 2, 32, 2.75))
    density = normal_values(key_list[1], (BASIS, BASIS), (AUX * BASIS * BASIS) ** -0.5, 0.00036621094, ((0, 32),))
    pair_mask = touch_ends((jax.random.randint(key_list[2], (NBLK, NBLK), 0, 4) < 3).astype(jnp.int32), jax.random.fold_in(key_list[2], 1), 0, 1)
    density_mask = touch_ends((jax.random.randint(key_list[3], (NBLK, NBLK), 0, 4) < 3).astype(jnp.int32), jax.random.fold_in(key_list[3], 1), 0, 1)
    return dict(three_centre=three_centre, density=density, pair_mask=pair_mask, density_mask=density_mask)


def expand(block_mask):
    widened = jnp.repeat(jnp.repeat(block_mask.astype(jnp.float32), BLK, axis=0), BLK, axis=1)
    return widened.astype(jnp.bfloat16)


def reference(three_centre, density, pair_mask, density_mask):
    masked_tensor = three_centre * expand(pair_mask).T[None, :, :]
    masked_density = density * expand(density_mask)

    def contract(running, aux_slab):
        half_built = jnp.dot(aux_slab.T, masked_density, preferred_element_type=jnp.float32).astype(jnp.bfloat16)
        return running + jnp.dot(half_built, aux_slab, preferred_element_type=jnp.float32), None

    running, _ = lax.scan(contract, jnp.zeros((BASIS, BASIS), jnp.float32), masked_tensor)
    return running
```

```python
import functools

import jax
import jax.numpy as jnp
from jax import lax
from jax.experimental import pallas as pl
from jax.experimental.pallas import tpu as pltpu
from jax.sharding import Mesh
from jax.sharding import PartitionSpec as P

VMEM = pltpu.VMEM
SMEM = pltpu.SMEM
AXES = ("y", "x", "z", "core")
ROW = ("y", "x")
COL = ("z", "core")
BLK = 64
HALF = 32
LANES = 128


def vmem():
    return pl.BlockSpec(memory_space=VMEM)


def smem():
    return pl.BlockSpec(memory_space=SMEM)


def prepare(tc_ref, den_ref, pair_ref, dmask_ref, keep_ref, send_ref, den_out_ref):
    row = lax.axis_index("y") * 4 + lax.axis_index("x")
    core = lax.axis_index("core")
    aux, height, basis = tc_ref.shape
    wide = 2 * LANES
    src = lax.broadcasted_iota(jnp.int32, (wide, wide), 0)
    dst = lax.broadcasted_iota(jnp.int32, (wide, wide), 1)
    half = jnp.where(dst < LANES, core, 1 - core)
    lane = dst % LANES
    block = lane // HALF
    hit = src == block * BLK + half * HALF + lane % HALF
    rows = tc_ref[...].reshape(aux * height, basis)
    for tile in range(basis // wide):
        s = [pair_ref[4 * tile + b, row].astype(jnp.float32) for b in range(4)]
        scale = jnp.where(block == 0, s[0], jnp.where(block == 1, s[1], jnp.where(block == 2, s[2], s[3])))
        pick = jnp.where(hit, scale, 0.0).astype(jnp.bfloat16)
        out = jnp.dot(rows[:, tile * wide : (tile + 1) * wide], pick, preferred_element_type=jnp.float32)
        out = out.astype(jnp.bfloat16).reshape(aux, height, wide)
        keep_ref[:, :, tile * LANES : (tile + 1) * LANES] = out[:, :, :LANES]
        send_ref[:, :, tile * LANES : (tile + 1) * LANES] = out[:, :, LANES:]
    mask_row = lax.axis_index("z")
    low = lax.broadcasted_iota(jnp.int32, (den_ref.shape[0], LANES), 1) < BLK
    for tile in range(basis // LANES):
        cols = slice(tile * LANES, (tile + 1) * LANES)
        a = dmask_ref[mask_row, 2 * tile].astype(jnp.float32)
        b = dmask_ref[mask_row, 2 * tile + 1].astype(jnp.float32)
        scaled = den_ref[:, cols].astype(jnp.float32) * jnp.where(low, a, b)
        den_out_ref[:, cols] = scaled.astype(jnp.bfloat16)


def contract(own_ref, other_ref, den_ref, out_ref):
    core = lax.axis_index("core")
    parts, height, width = own_ref.shape
    own = own_ref[...].reshape(parts * height, width)
    built = lax.dot_general(
        own, den_ref[...], (((0,), (0,)), ((), ())), preferred_element_type=jnp.float32
    ).astype(jnp.bfloat16)
    other = other_ref[...].reshape(parts * height, width)
    shape = (out_ref.shape[0], out_ref.shape[1], width)
    mine = jnp.dot(built, own, preferred_element_type=jnp.float32).astype(jnp.bfloat16)
    out_ref[:, :, pl.ds(pl.multiple_of(core * width, LANES), width)] = mine.reshape(shape)
    theirs = jnp.dot(built, other, preferred_element_type=jnp.float32).astype(jnp.bfloat16)
    out_ref[:, :, pl.ds(pl.multiple_of((1 - core) * width, LANES), width)] = theirs.reshape(shape)


def gather_groups(groups, start):
    return jnp.concatenate([g[:, start : start + HALF] for g in groups], axis=1)


def sum_aux(in_ref, out_ref):
    basis = in_ref.shape[2]
    for tile in range(basis // LANES):
        cols = slice(tile * LANES, (tile + 1) * LANES)
        total = in_ref[0, :, cols].astype(jnp.float32)
        for k in range(1, in_ref.shape[0]):
            total = total + in_ref[k, :, cols].astype(jnp.float32)
        groups = [total[8 * g : 8 * g + 8] for g in range(4)]
        for q in range(4):
            dest = ((tile % 4) * 4 + q) * 2 + tile // 4
            out_ref[dest] = gather_groups(groups, q * HALF)


def sum_planes(in_ref, out_ref):
    for core in range(2):
        total = in_ref[core]
        for z in range(1, in_ref.shape[0] // 2):
            total = total + in_ref[2 * z + core]
        for g in range(4):
            out_ref[core * HALF + 8 * g : core * HALF + 8 * g + 8, :] = total[:, g * HALF : (g + 1) * HALF]


def body(three_centre, density, pair_mask, density_mask):
    aux, height, basis = three_centre.shape
    width = basis // 2
    bf16, f32 = jnp.bfloat16, jnp.float32
    core = lax.axis_index("core")
    swap = [(0, 1), (1, 0)]
    half = jax.ShapeDtypeStruct((aux, height, width), bf16)
    keep, send, masked_density = pl.pallas_call(
        prepare,
        out_shape=(half, half, jax.ShapeDtypeStruct(density.shape, bf16)),
        in_specs=[vmem(), vmem(), smem(), smem()],
        out_specs=(vmem(), vmem(), vmem()),
        compiler_params=pltpu.CompilerParams(vmem_limit_bytes=32 << 20),
        name="prepare",
    )(three_centre, density, pair_mask, density_mask)
    full_density = lax.all_gather(masked_density, COL, axis=0, tiled=True)
    got = lax.ppermute(send, "core", swap)
    slabs = jnp.where(core == 0, jnp.concatenate([keep, got]), jnp.concatenate([got, keep]))
    own = lax.all_to_all(slabs, ROW, 0, 0, tiled=True)
    other = lax.ppermute(own, "core", swap)
    partial = pl.pallas_call(
        contract,
        out_shape=jax.ShapeDtypeStruct((2 * aux, HALF, basis), bf16),
        in_specs=[vmem(), vmem(), vmem()],
        out_specs=vmem(),
        compiler_params=pltpu.CompilerParams(vmem_limit_bytes=48 << 20),
        name="contract",
    )(own, other, full_density)
    pieces = lax.all_to_all(partial, ROW, 0, 0, tiled=True)
    packed = pl.pallas_call(
        sum_aux,
        out_shape=jax.ShapeDtypeStruct((32, 8, LANES), f32),
        in_specs=[vmem()],
        out_specs=vmem(),
        compiler_params=pltpu.CompilerParams(vmem_limit_bytes=16 << 20),
        name="sum_aux",
    )(pieces)
    arrived = lax.all_to_all(packed, COL, 0, 0, tiled=True)
    return pl.pallas_call(
        sum_planes,
        out_shape=jax.ShapeDtypeStruct((BLK, HALF), f32),
        in_specs=[vmem()],
        out_specs=vmem(),
        compiler_params=pltpu.CompilerParams(vmem_limit_bytes=16 << 20),
        name="sum_planes",
    )(arrived)


def solution(mesh):
    fine = Mesh(mesh.devices.reshape(4, 4, 16, 2), AXES)
    return jax.shard_map(
        body,
        mesh=fine,
        in_specs=(P(COL, ROW, None), P(COL, None), P(), P()),
        out_specs=P(ROW, COL),
        check_vma=False,
    )
```

```python
import jax
import jax.numpy as jnp
from jax import lax
from jax.experimental import pallas as pl
from jax.experimental.pallas import tpu as pltpu
from jax.sharding import Mesh
from jax.sharding import PartitionSpec as P

VMEM = pltpu.VMEM
SMEM = pltpu.SMEM
AXES = ("y", "x", "z", "core")
ROW = ("y", "x")
COL = ("z", "core")
BLK = 64
HALF = 32
LANES = 128
PACK = 16


def vmem():
    return pl.BlockSpec(memory_space=VMEM)


def smem():
    return pl.BlockSpec(memory_space=SMEM)


def first_density(den_hbm, dmask_hbm, piece_ref, den, dmask, sems):
    row = lax.axis_index("y") * 4 + lax.axis_index("x")
    tiles = den_hbm.shape[1] // LANES
    tile = row % tiles
    part = row // tiles
    source = den_hbm.at[
        pl.ds(pl.multiple_of(part * PACK, PACK), PACK), pl.ds(pl.multiple_of(tile * LANES, LANES), LANES)
    ]
    fetch_den = pltpu.make_async_copy(source, den, sems.at[0])
    fetch_mask = pltpu.make_async_copy(dmask_hbm, dmask, sems.at[1])
    fetch_den.start()
    fetch_mask.start()
    fetch_mask.wait()
    fetch_den.wait()
    low = lax.broadcasted_iota(jnp.int32, (PACK, LANES), 1) < BLK
    mask_row = lax.axis_index("z")
    a = dmask[mask_row, 2 * tile].astype(jnp.float32)
    b = dmask[mask_row, 2 * tile + 1].astype(jnp.float32)
    scaled = (den[...].astype(jnp.float32) * jnp.where(low, a, b)).astype(jnp.bfloat16)
    piece_ref[...] = jnp.broadcast_to(scaled[None], piece_ref.shape)


def prepare(tc_ref, pair_ref, keep_ref, send_ref):
    row = lax.axis_index("y") * 4 + lax.axis_index("x")
    core = lax.axis_index("core")
    aux, height, basis = tc_ref.shape
    wide = 2 * LANES
    src = lax.broadcasted_iota(jnp.int32, (wide, wide), 0)
    dst = lax.broadcasted_iota(jnp.int32, (wide, wide), 1)
    half = jnp.where(dst < LANES, core, 1 - core)
    lane = dst % LANES
    block = lane // HALF
    hit = src == block * BLK + half * HALF + lane % HALF
    rows = tc_ref[...].reshape(aux * height, basis)
    for tile in range(basis // wide):
        s = [pair_ref[4 * tile + b, row].astype(jnp.float32) for b in range(4)]
        scale = jnp.where(block == 0, s[0], jnp.where(block == 1, s[1], jnp.where(block == 2, s[2], s[3])))
        pick = jnp.where(hit, scale, 0.0).astype(jnp.bfloat16)
        out = jnp.dot(rows[:, tile * wide : (tile + 1) * wide], pick, preferred_element_type=jnp.float32)
        out = out.astype(jnp.bfloat16).reshape(aux, height, wide)
        keep_ref[:, :, tile * LANES : (tile + 1) * LANES] = out[:, :, :LANES]
        send_ref[:, :, tile * LANES : (tile + 1) * LANES] = out[:, :, LANES:]


def pack(keep_ref, got_ref, den_ref, out_ref):
    core = lax.axis_index("core")
    aux, height, width = keep_ref.shape
    out_ref[pl.ds(core * aux, aux), :height, :] = keep_ref[...]
    out_ref[pl.ds((1 - core) * aux, aux), :height, :] = got_ref[...]
    groups = width // LANES
    each = den_ref.shape[0] // groups
    for g in range(groups):
        part = den_ref[each * g : each * (g + 1)].reshape(each * PACK, LANES)
        spread = jnp.broadcast_to(part[None], (2 * aux, each * PACK, LANES))
        out_ref[:, height:, g * LANES : (g + 1) * LANES] = spread


def contract(own_ref, other_ref, out_ref, den):
    core = lax.axis_index("core")
    parts, both, width = own_ref.shape
    height = both // 2
    tiles = den.shape[-1] // LANES
    groups = width // LANES
    each = den.shape[0] // groups
    for ref, side in ((own_ref, core), (other_ref, 1 - core)):
        for k in range(2 * tiles):
            cols = slice(k % tiles * LANES, (k % tiles + 1) * LANES)
            for g in range(groups):
                part = ref[k, height:, g * LANES : (g + 1) * LANES].reshape(each, PACK, LANES)
                den[each * g : each * (g + 1), side, k // tiles, :, cols] = part
    own = own_ref[:, :height, :].reshape(parts * height, width)
    density = den[...].reshape(parts * height, den.shape[-1])
    built = lax.dot_general(
        own, density, (((0,), (0,)), ((), ())), preferred_element_type=jnp.float32
    ).astype(jnp.bfloat16)
    other = other_ref[:, :height, :].reshape(parts * height, width)
    shape = (out_ref.shape[0], out_ref.shape[1], width)
    mine = jnp.dot(built, own, preferred_element_type=jnp.float32).astype(jnp.bfloat16)
    out_ref[:, :, pl.ds(pl.multiple_of(core * width, LANES), width)] = mine.reshape(shape)
    theirs = jnp.dot(built, other, preferred_element_type=jnp.float32).astype(jnp.bfloat16)
    out_ref[:, :, pl.ds(pl.multiple_of((1 - core) * width, LANES), width)] = theirs.reshape(shape)


def gather_groups(groups, start):
    return jnp.concatenate([g[:, start : start + HALF] for g in groups], axis=1)


def sum_aux(in_ref, out_ref):
    basis = in_ref.shape[2]
    for tile in range(basis // LANES):
        cols = slice(tile * LANES, (tile + 1) * LANES)
        total = in_ref[0, :, cols].astype(jnp.float32)
        for k in range(1, in_ref.shape[0]):
            total = total + in_ref[k, :, cols].astype(jnp.float32)
        groups = [total[8 * g : 8 * g + 8] for g in range(4)]
        for q in range(4):
            dest = ((tile % 4) * 4 + q) * 2 + tile // 4
            out_ref[dest] = gather_groups(groups, q * HALF)


def sum_planes(in_ref, out_ref):
    totals = []
    for core in range(2):
        total = in_ref[core]
        for z in range(1, in_ref.shape[0] // 2):
            total = total + in_ref[2 * z + core]
        totals += [total[:, g * HALF : (g + 1) * HALF] for g in range(4)]
    out_ref[...] = jnp.concatenate(totals, axis=0).T


def body(three_centre, density, pair_mask, density_mask):
    aux, height, basis = three_centre.shape
    width = basis // 2
    bf16, f32 = jnp.bfloat16, jnp.float32
    swap = [(0, 1), (1, 0)]
    planes = 16
    piece = pl.pallas_call(
        first_density,
        out_shape=jax.ShapeDtypeStruct((planes, PACK, LANES), bf16),
        in_specs=[pl.BlockSpec(memory_space=pltpu.HBM)] * 2,
        out_specs=vmem(),
        scratch_shapes=[
            VMEM((PACK, LANES), bf16),
            SMEM(density_mask.shape, jnp.int32),
            pltpu.SemaphoreType.DMA((2,)),
        ],
        compiler_params=pltpu.CompilerParams(vmem_limit_bytes=60 << 20),
        name="first_density",
    )(density, density_mask)
    piece, three_centre = lax.optimization_barrier((piece, three_centre))
    along_z = lax.all_to_all(piece, "z", 0, 0, tiled=True)
    half = jax.ShapeDtypeStruct((aux, height, width), bf16)
    keep, send = pl.pallas_call(
        prepare,
        out_shape=(half, half),
        in_specs=[vmem(), smem()],
        out_specs=(vmem(), vmem()),
        compiler_params=pltpu.CompilerParams(vmem_limit_bytes=32 << 20),
        cost_estimate=pl.CostEstimate(flops=4 << 30, bytes_accessed=8 << 20, transcendentals=0),
        name="prepare",
    )(three_centre, pair_mask)
    along_z, send = lax.optimization_barrier((along_z, send))
    got = lax.ppermute(send, "core", swap)
    slabs = pl.pallas_call(
        pack,
        out_shape=jax.ShapeDtypeStruct((2 * aux, 2 * height, width), bf16),
        in_specs=[vmem()] * 3,
        out_specs=vmem(),
        compiler_params=pltpu.CompilerParams(vmem_limit_bytes=32 << 20),
        name="pack",
    )(keep, got, along_z)
    own = lax.all_to_all(slabs, ROW, 0, 0, tiled=True)
    other = lax.ppermute(own, "core", swap)
    partial = pl.pallas_call(
        contract,
        out_shape=jax.ShapeDtypeStruct((2 * aux, HALF, basis), bf16),
        in_specs=[vmem()] * 2,
        out_specs=vmem(),
        scratch_shapes=[VMEM((planes, 2, 2, PACK, basis), bf16)],
        compiler_params=pltpu.CompilerParams(vmem_limit_bytes=40 << 20),
        name="contract",
    )(own, other)
    pieces = lax.all_to_all(partial, ROW, 0, 0, tiled=True)
    packed = pl.pallas_call(
        sum_aux,
        out_shape=jax.ShapeDtypeStruct((32, 8, LANES), f32),
        in_specs=[vmem()],
        out_specs=vmem(),
        compiler_params=pltpu.CompilerParams(vmem_limit_bytes=16 << 20),
        name="sum_aux",
    )(pieces)
    arrived = lax.all_to_all(packed, COL, 0, 0, tiled=True)
    return pl.pallas_call(
        sum_planes,
        out_shape=jax.ShapeDtypeStruct((HALF, BLK), f32),
        in_specs=[vmem()],
        out_specs=vmem(),
        compiler_params=pltpu.CompilerParams(vmem_limit_bytes=16 << 20),
        name="sum_planes",
    )(arrived).T


def solution(mesh):
    fine = Mesh(mesh.devices.reshape(4, 4, 16, 2), AXES)
    return jax.shard_map(
        body,
        mesh=fine,
        in_specs=(P(COL, ROW, None), P(COL, None), P(), P()),
        out_specs=P(ROW, COL),
        check_vma=False,
    )
```

```python
import jax
import jax.numpy as jnp
from jax import lax
from jax.experimental import pallas as pl
from jax.experimental.pallas import tpu as pltpu
from jax.sharding import Mesh
from jax.sharding import PartitionSpec as P

VMEM = pltpu.VMEM
SMEM = pltpu.SMEM
AXES = ("y", "x", "z", "core")
ROW = ("y", "x")
COL = ("z", "core")
BLK = 64
HALF = 32
LANES = 128
PACK = 16


def vmem():
    return pl.BlockSpec(memory_space=VMEM)


def smem():
    return pl.BlockSpec(memory_space=SMEM)


def first_density(den_hbm, dmask_hbm, piece_ref, den, dmask, sems):
    row = lax.axis_index("y") * 4 + lax.axis_index("x")
    tiles = den_hbm.shape[1] // LANES
    tile = row % tiles
    part = row // tiles
    source = den_hbm.at[
        pl.ds(pl.multiple_of(part * PACK, PACK), PACK), pl.ds(pl.multiple_of(tile * LANES, LANES), LANES)
    ]
    fetch_den = pltpu.make_async_copy(source, den, sems.at[0])
    fetch_mask = pltpu.make_async_copy(dmask_hbm, dmask, sems.at[1])
    fetch_den.start()
    fetch_mask.start()
    fetch_mask.wait()
    fetch_den.wait()
    low = lax.broadcasted_iota(jnp.int32, (PACK, LANES), 1) < BLK
    mask_row = lax.axis_index("z")
    a = dmask[mask_row, 2 * tile].astype(jnp.float32)
    b = dmask[mask_row, 2 * tile + 1].astype(jnp.float32)
    scaled = (den[...].astype(jnp.float32) * jnp.where(low, a, b)).astype(jnp.bfloat16)
    piece_ref[...] = jnp.broadcast_to(scaled[None], piece_ref.shape)


def prepare(tc_ref, pair_ref, keep_ref, send_ref, last_ref):
    row = lax.axis_index("y") * 4 + lax.axis_index("x")
    core = lax.axis_index("core")
    aux, height, basis = tc_ref.shape
    wide = 2 * LANES
    src = lax.broadcasted_iota(jnp.int32, (wide, wide), 0)
    dst = lax.broadcasted_iota(jnp.int32, (wide, wide), 1)
    half = jnp.where(dst < LANES, core, 1 - core)
    lane = dst % LANES
    block = lane // HALF
    hit = src == block * BLK + half * HALF + lane % HALF
    rows = tc_ref[...].reshape(aux * height, basis)
    most = send_ref.shape[0]
    for tile in range(basis // wide):
        s = [pair_ref[4 * tile + b, row].astype(jnp.float32) for b in range(4)]
        scale = jnp.where(block == 0, s[0], jnp.where(block == 1, s[1], jnp.where(block == 2, s[2], s[3])))
        pick = jnp.where(hit, scale, 0.0).astype(jnp.bfloat16)
        out = jnp.dot(rows[:, tile * wide : (tile + 1) * wide], pick, preferred_element_type=jnp.float32)
        out = out.astype(jnp.bfloat16).reshape(aux, height, wide)
        keep_ref[:, :, tile * LANES : (tile + 1) * LANES] = out[:, :, :LANES]
        send_ref[:, :, tile * LANES : (tile + 1) * LANES] = out[:most, :, LANES:]
        last_ref[:, :, tile * LANES : (tile + 1) * LANES] = out[most:, :, LANES:]


def join(keep_ref, got_ref, last_ref, out_ref):
    core = lax.axis_index("core")
    aux = keep_ref.shape[0]
    most = got_ref.shape[0] // 2
    out_ref[pl.ds(core * aux, aux)] = keep_ref[...]
    out_ref[pl.ds((1 - core) * aux, most)] = got_ref[pl.ds((1 - core) * most, most)]
    out_ref[pl.ds((1 - core) * aux + most, aux - most)] = last_ref[pl.ds((1 - core) * (aux - most), aux - most)]


def pack(slab_ref, den_ref, out_ref):
    parts, height, width = slab_ref.shape
    out_ref[:, :height, :] = slab_ref[...]
    groups = width // LANES
    each = den_ref.shape[0] // groups
    for g in range(groups):
        part = den_ref[each * g : each * (g + 1)].reshape(each * PACK, LANES)
        spread = jnp.broadcast_to(part[None], (parts, each * PACK, LANES))
        out_ref[:, height:, g * LANES : (g + 1) * LANES] = spread


def contract(own_ref, other_ref, out_ref, den):
    core = lax.axis_index("core")
    parts, both, width = own_ref.shape
    height = both // 2
    tiles = den.shape[-1] // LANES
    groups = width // LANES
    each = den.shape[0] // groups
    for ref, side in ((own_ref, core), (other_ref, 1 - core)):
        for k in range(2 * tiles):
            cols = slice(k % tiles * LANES, (k % tiles + 1) * LANES)
            for g in range(groups):
                part = ref[k, height:, g * LANES : (g + 1) * LANES].reshape(each, PACK, LANES)
                den[each * g : each * (g + 1), side, k // tiles, :, cols] = part
    own = own_ref[:, :height, :].reshape(parts * height, width)
    density = den[...].reshape(parts * height, den.shape[-1])
    built = lax.dot_general(
        own, density, (((0,), (0,)), ((), ())), preferred_element_type=jnp.float32
    ).astype(jnp.bfloat16)
    other = other_ref[:, :height, :].reshape(parts * height, width)
    shape = (out_ref.shape[0], out_ref.shape[1], width)
    mine = jnp.dot(built, own, preferred_element_type=jnp.float32).astype(jnp.bfloat16)
    out_ref[:, :, pl.ds(pl.multiple_of(core * width, LANES), width)] = mine.reshape(shape)
    theirs = jnp.dot(built, other, preferred_element_type=jnp.float32).astype(jnp.bfloat16)
    out_ref[:, :, pl.ds(pl.multiple_of((1 - core) * width, LANES), width)] = theirs.reshape(shape)


def gather_groups(groups, start):
    return jnp.concatenate([g[:, start : start + HALF] for g in groups], axis=1)


def sum_aux(in_ref, out_ref):
    basis = in_ref.shape[2]
    for tile in range(basis // LANES):
        cols = slice(tile * LANES, (tile + 1) * LANES)
        total = in_ref[0, :, cols].astype(jnp.float32)
        for k in range(1, in_ref.shape[0]):
            total = total + in_ref[k, :, cols].astype(jnp.float32)
        groups = [total[8 * g : 8 * g + 8] for g in range(4)]
        for q in range(4):
            dest = ((tile % 4) * 4 + q) * 2 + tile // 4
            out_ref[dest] = gather_groups(groups, q * HALF)


def sum_planes(in_ref, out_ref):
    totals = []
    for core in range(2):
        total = in_ref[core]
        for z in range(1, in_ref.shape[0] // 2):
            total = total + in_ref[2 * z + core]
        totals += [total[:, g * HALF : (g + 1) * HALF] for g in range(4)]
    out_ref[...] = jnp.concatenate(totals, axis=0).T


def body(three_centre, density, pair_mask, density_mask):
    aux, height, basis = three_centre.shape
    width = basis // 2
    bf16, f32 = jnp.bfloat16, jnp.float32
    swap = [(0, 1), (1, 0)]
    planes = 16
    piece = pl.pallas_call(
        first_density,
        out_shape=jax.ShapeDtypeStruct((planes, PACK, LANES), bf16),
        in_specs=[pl.BlockSpec(memory_space=pltpu.HBM)] * 2,
        out_specs=vmem(),
        scratch_shapes=[
            VMEM((PACK, LANES), bf16),
            SMEM(density_mask.shape, jnp.int32),
            pltpu.SemaphoreType.DMA((2,)),
        ],
        compiler_params=pltpu.CompilerParams(vmem_limit_bytes=60 << 20),
        name="first_density",
    )(density, density_mask)
    piece, three_centre = lax.optimization_barrier((piece, three_centre))
    along_z = lax.all_to_all(piece, "z", 0, 0, tiled=True)
    half = jax.ShapeDtypeStruct((aux, height, width), bf16)
    most = jax.ShapeDtypeStruct((aux - 1, height, width), bf16)
    last = jax.ShapeDtypeStruct((1, height, width), bf16)
    keep, send, send_last = pl.pallas_call(
        prepare,
        out_shape=(half, most, last),
        in_specs=[vmem(), smem()],
        out_specs=(vmem(), vmem(), vmem()),
        compiler_params=pltpu.CompilerParams(vmem_limit_bytes=32 << 20),
        cost_estimate=pl.CostEstimate(flops=4 << 30, bytes_accessed=8 << 20, transcendentals=0),
        name="prepare",
    )(three_centre, pair_mask)
    got = lax.all_gather(send, "core", axis=0, tiled=True)
    got_last = lax.all_gather(send_last, "core", axis=0, tiled=True)
    both = pl.pallas_call(
        join,
        out_shape=jax.ShapeDtypeStruct((2 * aux, height, width), bf16),
        in_specs=[vmem()] * 3,
        out_specs=vmem(),
        compiler_params=pltpu.CompilerParams(vmem_limit_bytes=32 << 20),
        name="join",
    )(keep, got, got_last)
    slabs = pl.pallas_call(
        pack,
        out_shape=jax.ShapeDtypeStruct((2 * aux, 2 * height, width), bf16),
        in_specs=[vmem()] * 2,
        out_specs=vmem(),
        compiler_params=pltpu.CompilerParams(vmem_limit_bytes=32 << 20),
        name="pack",
    )(both, along_z)
    own = lax.all_to_all(slabs, ROW, 0, 0, tiled=True)
    other = lax.ppermute(own, "core", swap)
    partial = pl.pallas_call(
        contract,
        out_shape=jax.ShapeDtypeStruct((2 * aux, HALF, basis), bf16),
        in_specs=[vmem()] * 2,
        out_specs=vmem(),
        scratch_shapes=[VMEM((planes, 2, 2, PACK, basis), bf16)],
        compiler_params=pltpu.CompilerParams(vmem_limit_bytes=40 << 20),
        name="contract",
    )(own, other)
    pieces = lax.all_to_all(partial, ROW, 0, 0, tiled=True)
    packed = pl.pallas_call(
        sum_aux,
        out_shape=jax.ShapeDtypeStruct((32, 8, LANES), f32),
        in_specs=[vmem()],
        out_specs=vmem(),
        compiler_params=pltpu.CompilerParams(vmem_limit_bytes=16 << 20),
        name="sum_aux",
    )(pieces)
    arrived = lax.all_to_all(packed, COL, 0, 0, tiled=True)
    return pl.pallas_call(
        sum_planes,
        out_shape=jax.ShapeDtypeStruct((HALF, BLK), f32),
        in_specs=[vmem()],
        out_specs=vmem(),
        compiler_params=pltpu.CompilerParams(vmem_limit_bytes=16 << 20),
        name="sum_planes",
    )(arrived).T


def solution(mesh):
    fine = Mesh(mesh.devices.reshape(4, 4, 16, 2), AXES)
    return jax.shard_map(
        body,
        mesh=fine,
        in_specs=(P(COL, ROW, None), P(COL, None), P(), P()),
        out_specs=P(ROW, COL),
        check_vma=False,
    )
```

```python
import jax
import jax.numpy as jnp
from jax import lax
from jax.experimental import pallas as pl
from jax.experimental.pallas import tpu as pltpu
from jax.sharding import Mesh
from jax.sharding import PartitionSpec as P

VMEM = pltpu.VMEM
SMEM = pltpu.SMEM
AXES = ("y", "x", "z", "core")
ROW = ("y", "x")
COL = ("z", "core")
BLK = 64
HALF = 32
LANES = 128
PACK = 16
PLANES = 16
TURN = PLANES // 2
ROWS = 16
SHIFT = 10


def vmem():
    return pl.BlockSpec(memory_space=VMEM)


def smem():
    return pl.BlockSpec(memory_space=SMEM)


def first_density(den_hbm, dmask_hbm, piece_ref, den, dmask, sems):
    row = lax.axis_index("y") * 4 + lax.axis_index("x")
    tiles = den_hbm.shape[1] // LANES
    tile = row % tiles
    part = row // tiles
    source = den_hbm.at[
        pl.ds(pl.multiple_of(part * PACK, PACK), PACK), pl.ds(pl.multiple_of(tile * LANES, LANES), LANES)
    ]
    fetch_den = pltpu.make_async_copy(source, den, sems.at[0])
    fetch_mask = pltpu.make_async_copy(dmask_hbm, dmask, sems.at[1])
    fetch_den.start()
    fetch_mask.start()
    fetch_mask.wait()
    fetch_den.wait()
    low = lax.broadcasted_iota(jnp.int32, (PACK, LANES), 1) < BLK
    mask_row = lax.axis_index("z")
    a = dmask[mask_row, 2 * tile].astype(jnp.float32)
    b = dmask[mask_row, 2 * tile + 1].astype(jnp.float32)
    scaled = (den[...].astype(jnp.float32) * jnp.where(low, a, b)).astype(jnp.bfloat16)
    piece_ref[...] = jnp.broadcast_to(scaled[None], piece_ref.shape)


def prepare(tc_ref, pair_ref, keep_ref, send_ref, last_ref):
    row = lax.axis_index("y") * 4 + lax.axis_index("x")
    core = lax.axis_index("core")
    aux, height, basis = tc_ref.shape
    wide = 2 * LANES
    src = lax.broadcasted_iota(jnp.int32, (wide, wide), 0)
    dst = lax.broadcasted_iota(jnp.int32, (wide, wide), 1)
    half = jnp.where(dst < LANES, core, 1 - core)
    lane = dst % LANES
    block = lane // HALF
    hit = src == block * BLK + half * HALF + lane % HALF
    rows = tc_ref[...].reshape(aux * height, basis)
    most = send_ref.shape[0]
    for tile in range(basis // wide):
        s = [pair_ref[4 * tile + b, row].astype(jnp.float32) for b in range(4)]
        scale = jnp.where(block == 0, s[0], jnp.where(block == 1, s[1], jnp.where(block == 2, s[2], s[3])))
        pick = jnp.where(hit, scale, 0.0).astype(jnp.bfloat16)
        out = jnp.dot(rows[:, tile * wide : (tile + 1) * wide], pick, preferred_element_type=jnp.float32)
        out = out.astype(jnp.bfloat16).reshape(aux, height, wide)
        keep_ref[:, :, tile * LANES : (tile + 1) * LANES] = out[:, :, :LANES]
        send_ref[:, :, tile * LANES : (tile + 1) * LANES] = out[:most, :, LANES:]
        last_ref[:, :, tile * LANES : (tile + 1) * LANES] = out[most:, :, LANES:]


def join(keep_ref, got_ref, last_ref, out_ref):
    core = lax.axis_index("core")
    aux = keep_ref.shape[0]
    most = got_ref.shape[0] // 2
    out_ref[pl.ds(core * aux, aux)] = keep_ref[...]
    out_ref[pl.ds((1 - core) * aux, most)] = got_ref[pl.ds((1 - core) * most, most)]
    out_ref[pl.ds((1 - core) * aux + most, aux - most)] = last_ref[pl.ds((1 - core) * (aux - most), aux - most)]


def pack(slab_ref, den_ref, out_ref):
    parts, height, width = slab_ref.shape
    out_ref[:, :height, :] = slab_ref[...]
    groups = width // LANES
    each = den_ref.shape[0] // groups
    for g in range(groups):
        slot = (each * g + TURN) % PLANES
        part = den_ref[slot : slot + each].reshape(each * PACK, LANES)
        spread = jnp.broadcast_to(part[None], (parts, each * PACK, LANES))
        out_ref[:, height:, g * LANES : (g + 1) * LANES] = spread


def contract(own_ref, other_ref, out_ref, den):
    core = lax.axis_index("core")
    parts, both, width = own_ref.shape
    height = both // 2
    tiles = den.shape[-1] // LANES
    groups = width // LANES
    each = den.shape[0] // groups
    for ref, side in ((own_ref, core), (other_ref, 1 - core)):
        for k in range(ROWS):
            row = (k + SHIFT) % ROWS
            cols = slice(row % tiles * LANES, (row % tiles + 1) * LANES)
            for g in range(groups):
                part = ref[k, height:, g * LANES : (g + 1) * LANES].reshape(each, PACK, LANES)
                den[each * g : each * (g + 1), side, row // tiles, :, cols] = part

    def slab(ref):
        turned = jnp.concatenate([ref[ROWS - SHIFT :, :height, :], ref[: ROWS - SHIFT, :height, :]])
        return turned.reshape(parts * height, width)

    def put(value, cols):
        value = value.astype(jnp.bfloat16).reshape(ROWS, out_ref.shape[1], width)
        out_ref[: ROWS - SHIFT, :, cols] = value[SHIFT:]
        out_ref[ROWS - SHIFT :, :, cols] = value[:SHIFT]

    own = slab(own_ref)
    density = den[...].reshape(parts * height, den.shape[-1])
    built = lax.dot_general(
        own, density, (((0,), (0,)), ((), ())), preferred_element_type=jnp.float32
    ).astype(jnp.bfloat16)
    put(jnp.dot(built, own, preferred_element_type=jnp.float32), pl.ds(pl.multiple_of(core * width, LANES), width))
    put(
        jnp.dot(built, slab(other_ref), preferred_element_type=jnp.float32),
        pl.ds(pl.multiple_of((1 - core) * width, LANES), width),
    )


def gather_groups(groups, start):
    return jnp.concatenate([g[:, start : start + HALF] for g in groups], axis=1)


def sum_aux(in_ref, out_ref):
    basis = in_ref.shape[2]
    for tile in range(basis // LANES):
        cols = slice(tile * LANES, (tile + 1) * LANES)
        total = in_ref[0, :, cols].astype(jnp.float32)
        for k in range(1, in_ref.shape[0]):
            total = total + in_ref[k, :, cols].astype(jnp.float32)
        groups = [total[8 * g : 8 * g + 8] for g in range(4)]
        for q in range(4):
            dest = ((tile % 4 * 4 + q + TURN) % PLANES) * 2 + tile // 4
            out_ref[dest] = gather_groups(groups, q * HALF)


def sum_planes(in_ref, out_ref):
    totals = []
    for core in range(2):
        total = in_ref[core]
        for z in range(1, in_ref.shape[0] // 2):
            total = total + in_ref[2 * z + core]
        totals += [total[:, g * HALF : (g + 1) * HALF] for g in range(4)]
    out_ref[...] = jnp.concatenate(totals, axis=0).T


def body(three_centre, density, pair_mask, density_mask):
    aux, height, basis = three_centre.shape
    width = basis // 2
    bf16, f32 = jnp.bfloat16, jnp.float32
    swap = [(0, 1), (1, 0)]
    planes = PLANES
    piece = pl.pallas_call(
        first_density,
        out_shape=jax.ShapeDtypeStruct((planes, PACK, LANES), bf16),
        in_specs=[pl.BlockSpec(memory_space=pltpu.HBM)] * 2,
        out_specs=vmem(),
        scratch_shapes=[
            VMEM((PACK, LANES), bf16),
            SMEM(density_mask.shape, jnp.int32),
            pltpu.SemaphoreType.DMA((2,)),
        ],
        compiler_params=pltpu.CompilerParams(vmem_limit_bytes=60 << 20),
        name="first_density",
    )(density, density_mask)
    piece, three_centre = lax.optimization_barrier((piece, three_centre))
    turned = [(i + TURN) % PLANES for i in range(PLANES)]
    along_z = lax.all_to_all(piece, "z", 0, 0, axis_index_groups=[turned], tiled=True)
    half = jax.ShapeDtypeStruct((aux, height, width), bf16)
    most = jax.ShapeDtypeStruct((aux - 1, height, width), bf16)
    last = jax.ShapeDtypeStruct((1, height, width), bf16)
    keep, send, send_last = pl.pallas_call(
        prepare,
        out_shape=(half, most, last),
        in_specs=[vmem(), smem()],
        out_specs=(vmem(), vmem(), vmem()),
        compiler_params=pltpu.CompilerParams(vmem_limit_bytes=32 << 20),
        cost_estimate=pl.CostEstimate(flops=4 << 30, bytes_accessed=8 << 20, transcendentals=0),
        name="prepare",
    )(three_centre, pair_mask)
    got = lax.all_gather(send, "core", axis=0, tiled=True)
    got_last = lax.all_gather(send_last, "core", axis=0, tiled=True)
    both = pl.pallas_call(
        join,
        out_shape=jax.ShapeDtypeStruct((2 * aux, height, width), bf16),
        in_specs=[vmem()] * 3,
        out_specs=vmem(),
        compiler_params=pltpu.CompilerParams(vmem_limit_bytes=32 << 20),
        name="join",
    )(keep, got, got_last)
    slabs = pl.pallas_call(
        pack,
        out_shape=jax.ShapeDtypeStruct((2 * aux, 2 * height, width), bf16),
        in_specs=[vmem()] * 2,
        out_specs=vmem(),
        compiler_params=pltpu.CompilerParams(vmem_limit_bytes=32 << 20),
        name="pack",
    )(both, along_z)
    from_corner = [[(i + SHIFT) % ROWS for i in range(ROWS)]]
    own = lax.all_to_all(slabs, ROW, 0, 0, axis_index_groups=from_corner, tiled=True)
    other = lax.ppermute(own, "core", swap)
    partial = pl.pallas_call(
        contract,
        out_shape=jax.ShapeDtypeStruct((2 * aux, HALF, basis), bf16),
        in_specs=[vmem()] * 2,
        out_specs=vmem(),
        scratch_shapes=[VMEM((planes, 2, 2, PACK, basis), bf16)],
        compiler_params=pltpu.CompilerParams(vmem_limit_bytes=40 << 20),
        name="contract",
    )(own, other)
    pieces = lax.all_to_all(partial, ROW, 0, 0, axis_index_groups=from_corner, tiled=True)
    packed = pl.pallas_call(
        sum_aux,
        out_shape=jax.ShapeDtypeStruct((32, 8, LANES), f32),
        in_specs=[vmem()],
        out_specs=vmem(),
        compiler_params=pltpu.CompilerParams(vmem_limit_bytes=16 << 20),
        name="sum_aux",
    )(pieces)
    pairs = [[2 * z + c for z in turned for c in range(2)]]
    arrived = lax.all_to_all(packed, COL, 0, 0, axis_index_groups=pairs, tiled=True)
    return pl.pallas_call(
        sum_planes,
        out_shape=jax.ShapeDtypeStruct((HALF, BLK), f32),
        in_specs=[vmem()],
        out_specs=vmem(),
        compiler_params=pltpu.CompilerParams(vmem_limit_bytes=16 << 20),
        name="sum_planes",
    )(arrived).T


def solution(mesh):
    fine = Mesh(mesh.devices.reshape(4, 4, 16, 2), AXES)
    return jax.shard_map(
        body,
        mesh=fine,
        in_specs=(P(COL, ROW, None), P(COL, None), P(), P()),
        out_specs=P(ROW, COL),
        check_vma=False,
    )
```

```python
import jax
import jax.numpy as jnp
from jax import lax
from jax.experimental import pallas as pl
from jax.experimental.pallas import tpu as pltpu
from jax.sharding import Mesh
from jax.sharding import PartitionSpec as P

VMEM = pltpu.VMEM
SMEM = pltpu.SMEM
AXES = ("y", "x", "z", "core")
ROW = ("y", "x")
COL = ("z", "core")
BLK = 64
HALF = 32
LANES = 128
PACK = 16
PLANES = 16
TURN = PLANES // 2
ROWS = 16
SHIFT = 10


def vmem():
    return pl.BlockSpec(memory_space=VMEM)


def smem():
    return pl.BlockSpec(memory_space=SMEM)


def prepare(
    tc_hbm, den_hbm, pair_hbm, dmask_hbm, piece_ref, keep_ref, send_ref, last_ref, tc, den, pair, dmask, sems
):
    row = lax.axis_index("y") * 4 + lax.axis_index("x")
    core = lax.axis_index("core")
    aux, height, basis = tc.shape
    tiles = basis // LANES
    tile = row % tiles
    part = row // tiles
    piece = den_hbm.at[
        pl.ds(pl.multiple_of(part * PACK, PACK), PACK), pl.ds(pl.multiple_of(tile * LANES, LANES), LANES)
    ]
    moves = [(pair_hbm, pair), (dmask_hbm, dmask), (piece, den)]
    moves += [(tc_hbm.at[k], tc.at[k]) for k in range(aux)]
    copies = [pltpu.make_async_copy(src, dst, sems.at[k]) for k, (src, dst) in enumerate(moves)]
    for copy in copies:
        copy.start()
    wide = 2 * LANES
    src = lax.broadcasted_iota(jnp.int32, (wide, wide), 0)
    dst = lax.broadcasted_iota(jnp.int32, (wide, wide), 1)
    half = jnp.where(dst < LANES, core, 1 - core)
    lane = dst % LANES
    block = lane // HALF
    hit = src == block * BLK + half * HALF + lane % HALF
    for copy in copies[:3]:
        copy.wait()
    low = lax.broadcasted_iota(jnp.int32, (PACK, LANES), 1) < BLK
    mask_row = lax.axis_index("z")
    a = dmask[mask_row, 2 * tile].astype(jnp.float32)
    b = dmask[mask_row, 2 * tile + 1].astype(jnp.float32)
    scaled = (den[...].astype(jnp.float32) * jnp.where(low, a, b)).astype(jnp.bfloat16)
    piece_ref[...] = jnp.broadcast_to(scaled[None], piece_ref.shape)
    picks = []
    for t in range(basis // wide):
        s = [pair[4 * t + b, row].astype(jnp.float32) for b in range(4)]
        scale = jnp.where(block == 0, s[0], jnp.where(block == 1, s[1], jnp.where(block == 2, s[2], s[3])))
        picks.append(jnp.where(hit, scale, 0.0).astype(jnp.bfloat16))
    most = send_ref.shape[0]
    step = 2
    for k in range(0, aux, step):
        for copy in copies[3 + k : 3 + k + step]:
            copy.wait()
        rows = tc[k : k + step].reshape(step * height, basis)
        for t, pick in enumerate(picks):
            cols = slice(t * LANES, (t + 1) * LANES)
            out = jnp.dot(rows[:, t * wide : (t + 1) * wide], pick, preferred_element_type=jnp.float32)
            out = out.astype(jnp.bfloat16).reshape(step, height, wide)
            keep_ref[k : k + step, :, cols] = out[:, :, :LANES]
            inside = min(step, most - k)
            send_ref[k : k + inside, :, cols] = out[:inside, :, LANES:]
            if inside < step:
                last_ref[:, :, cols] = out[inside:, :, LANES:]


def join(keep_ref, got_ref, last_ref, out_ref):
    core = lax.axis_index("core")
    aux = keep_ref.shape[0]
    most = got_ref.shape[0] // 2
    out_ref[pl.ds(core * aux, aux)] = keep_ref[...]
    out_ref[pl.ds((1 - core) * aux, most)] = got_ref[pl.ds((1 - core) * most, most)]
    out_ref[pl.ds((1 - core) * aux + most, aux - most)] = last_ref[pl.ds((1 - core) * (aux - most), aux - most)]


def pack(slab_ref, den_ref, out_ref):
    parts, height, width = slab_ref.shape
    out_ref[:, :height, :] = slab_ref[...]
    groups = width // LANES
    each = den_ref.shape[0] // groups
    for g in range(groups):
        slot = (each * g + TURN) % PLANES
        part = den_ref[slot : slot + each].reshape(each * PACK, LANES)
        spread = jnp.broadcast_to(part[None], (parts, each * PACK, LANES))
        out_ref[:, height:, g * LANES : (g + 1) * LANES] = spread


def contract(own_ref, other_ref, out_ref, den):
    core = lax.axis_index("core")
    parts, both, width = own_ref.shape
    height = both // 2
    tiles = den.shape[-1] // LANES
    groups = width // LANES
    each = den.shape[0] // groups
    for ref, side in ((own_ref, core), (other_ref, 1 - core)):
        for k in range(ROWS):
            row = (k + SHIFT) % ROWS
            cols = slice(row % tiles * LANES, (row % tiles + 1) * LANES)
            for g in range(groups):
                part = ref[k, height:, g * LANES : (g + 1) * LANES].reshape(each, PACK, LANES)
                den[each * g : each * (g + 1), side, row // tiles, :, cols] = part

    def slab(ref):
        turned = jnp.concatenate([ref[ROWS - SHIFT :, :height, :], ref[: ROWS - SHIFT, :height, :]])
        return turned.reshape(parts * height, width)

    def put(value, cols):
        value = value.astype(jnp.bfloat16).reshape(ROWS, out_ref.shape[1], width)
        out_ref[: ROWS - SHIFT, :, cols] = value[SHIFT:]
        out_ref[ROWS - SHIFT :, :, cols] = value[:SHIFT]

    own = slab(own_ref)
    density = den[...].reshape(parts * height, den.shape[-1])
    built = lax.dot_general(
        own, density, (((0,), (0,)), ((), ())), preferred_element_type=jnp.float32
    ).astype(jnp.bfloat16)
    put(jnp.dot(built, own, preferred_element_type=jnp.float32), pl.ds(pl.multiple_of(core * width, LANES), width))
    put(
        jnp.dot(built, slab(other_ref), preferred_element_type=jnp.float32),
        pl.ds(pl.multiple_of((1 - core) * width, LANES), width),
    )


def gather_groups(groups, start):
    return jnp.concatenate([g[:, start : start + HALF] for g in groups], axis=1)


def sum_aux(in_ref, out_ref):
    basis = in_ref.shape[2]
    for tile in range(basis // LANES):
        cols = slice(tile * LANES, (tile + 1) * LANES)
        total = in_ref[0, :, cols].astype(jnp.float32)
        for k in range(1, in_ref.shape[0]):
            total = total + in_ref[k, :, cols].astype(jnp.float32)
        groups = [total[8 * g : 8 * g + 8] for g in range(4)]
        for q in range(4):
            dest = ((tile % 4 * 4 + q + TURN) % PLANES) * 2 + tile // 4
            out_ref[dest] = gather_groups(groups, q * HALF)


def sum_planes(in_ref, out_ref):
    totals = []
    for core in range(2):
        total = in_ref[core]
        for z in range(1, in_ref.shape[0] // 2):
            total = total + in_ref[2 * z + core]
        totals += [total[:, g * HALF : (g + 1) * HALF] for g in range(4)]
    out_ref[...] = jnp.concatenate(totals, axis=0).T


def body(three_centre, density, pair_mask, density_mask):
    aux, height, basis = three_centre.shape
    width = basis // 2
    bf16, f32 = jnp.bfloat16, jnp.float32
    swap = [(0, 1), (1, 0)]
    planes = PLANES
    half = jax.ShapeDtypeStruct((aux, height, width), bf16)
    most = jax.ShapeDtypeStruct((aux - 1, height, width), bf16)
    last = jax.ShapeDtypeStruct((1, height, width), bf16)
    piece, keep, send, send_last = pl.pallas_call(
        prepare,
        out_shape=(jax.ShapeDtypeStruct((planes, PACK, LANES), bf16), half, most, last),
        in_specs=[pl.BlockSpec(memory_space=pltpu.HBM)] * 4,
        out_specs=(vmem(),) * 4,
        scratch_shapes=[
            VMEM(three_centre.shape, bf16),
            VMEM((PACK, LANES), bf16),
            SMEM(pair_mask.shape, jnp.int32),
            SMEM(density_mask.shape, jnp.int32),
            pltpu.SemaphoreType.DMA((3 + aux,)),
        ],
        compiler_params=pltpu.CompilerParams(vmem_limit_bytes=40 << 20),
        name="prepare",
    )(*(pltpu.with_memory_space_constraint(a, pltpu.HBM) for a in (three_centre, density, pair_mask, density_mask)))
    turned = [(i + TURN) % PLANES for i in range(PLANES)]
    along_z = lax.all_to_all(piece, "z", 0, 0, axis_index_groups=[turned], tiled=True)
    got = lax.all_gather(send, "core", axis=0, tiled=True)
    got_last = lax.all_gather(send_last, "core", axis=0, tiled=True)
    both = pl.pallas_call(
        join,
        out_shape=jax.ShapeDtypeStruct((2 * aux, height, width), bf16),
        in_specs=[vmem()] * 3,
        out_specs=vmem(),
        compiler_params=pltpu.CompilerParams(vmem_limit_bytes=32 << 20),
        name="join",
    )(keep, got, got_last)
    slabs = pl.pallas_call(
        pack,
        out_shape=jax.ShapeDtypeStruct((2 * aux, 2 * height, width), bf16),
        in_specs=[vmem()] * 2,
        out_specs=vmem(),
        compiler_params=pltpu.CompilerParams(vmem_limit_bytes=32 << 20),
        name="pack",
    )(both, along_z)
    from_corner = [[(i + SHIFT) % ROWS for i in range(ROWS)]]
    own = lax.all_to_all(slabs, ROW, 0, 0, axis_index_groups=from_corner, tiled=True)
    other = lax.ppermute(own, "core", swap)
    partial = pl.pallas_call(
        contract,
        out_shape=jax.ShapeDtypeStruct((2 * aux, HALF, basis), bf16),
        in_specs=[vmem()] * 2,
        out_specs=vmem(),
        scratch_shapes=[VMEM((planes, 2, 2, PACK, basis), bf16)],
        compiler_params=pltpu.CompilerParams(vmem_limit_bytes=40 << 20),
        name="contract",
    )(own, other)
    pieces = lax.all_to_all(partial, ROW, 0, 0, axis_index_groups=from_corner, tiled=True)
    packed = pl.pallas_call(
        sum_aux,
        out_shape=jax.ShapeDtypeStruct((32, 8, LANES), f32),
        in_specs=[vmem()],
        out_specs=vmem(),
        compiler_params=pltpu.CompilerParams(vmem_limit_bytes=16 << 20),
        name="sum_aux",
    )(pieces)
    pairs = [[2 * z + c for z in turned for c in range(2)]]
    arrived = lax.all_to_all(packed, COL, 0, 0, axis_index_groups=pairs, tiled=True)
    return pl.pallas_call(
        sum_planes,
        out_shape=jax.ShapeDtypeStruct((HALF, BLK), f32),
        in_specs=[vmem()],
        out_specs=vmem(),
        compiler_params=pltpu.CompilerParams(vmem_limit_bytes=16 << 20),
        name="sum_planes",
    )(arrived).T


def solution(mesh):
    fine = Mesh(mesh.devices.reshape(4, 4, 16, 2), AXES)
    return jax.shard_map(
        body,
        mesh=fine,
        in_specs=(P(COL, ROW, None), P(COL, None), P(), P()),
        out_specs=P(ROW, COL),
        check_vma=False,
    )
```

```python
import jax
import jax.numpy as jnp
from jax import lax
from jax.experimental import pallas as pl
from jax.experimental.pallas import tpu as pltpu
from jax.sharding import Mesh
from jax.sharding import PartitionSpec as P

VMEM = pltpu.VMEM
SMEM = pltpu.SMEM
AXES = ("y", "x", "z", "core")
ROW = ("y", "x")
COL = ("z", "core")
BLK = 64
HALF = 32
LANES = 128
PACK = 16
PLANES = 16
TURN = PLANES // 2
ROWS = 16
SHIFT = 10


def vmem():
    return pl.BlockSpec(memory_space=VMEM)


def smem():
    return pl.BlockSpec(memory_space=SMEM)


def prepare(
    tc_hbm, den_hbm, pair_hbm, dmask_hbm, piece_ref, keep_ref, send_ref, last_ref, tc, den, pair, dmask, sems
):
    row = lax.axis_index("y") * 4 + lax.axis_index("x")
    core = lax.axis_index("core")
    aux, height, basis = tc.shape
    tiles = basis // LANES
    tile = row % tiles
    part = row // tiles
    piece = den_hbm.at[
        pl.ds(pl.multiple_of(part * PACK, PACK), PACK), pl.ds(pl.multiple_of(tile * LANES, LANES), LANES)
    ]
    moves = [(pair_hbm, pair), (dmask_hbm, dmask), (piece, den)]
    moves += [(tc_hbm.at[k], tc.at[k]) for k in range(aux)]
    copies = [pltpu.make_async_copy(src, dst, sems.at[k]) for k, (src, dst) in enumerate(moves)]
    for copy in copies:
        copy.start()
    wide = 2 * LANES
    src = lax.broadcasted_iota(jnp.int32, (wide, wide), 0)
    dst = lax.broadcasted_iota(jnp.int32, (wide, wide), 1)
    half = jnp.where(dst < LANES, core, 1 - core)
    lane = dst % LANES
    block = lane // HALF
    hit = src == block * BLK + half * HALF + lane % HALF
    for copy in copies[:3]:
        copy.wait()
    low = lax.broadcasted_iota(jnp.int32, (PACK, LANES), 1) < BLK
    mask_row = lax.axis_index("z")
    a = dmask[mask_row, 2 * tile].astype(jnp.float32)
    b = dmask[mask_row, 2 * tile + 1].astype(jnp.float32)
    scaled = (den[...].astype(jnp.float32) * jnp.where(low, a, b)).astype(jnp.bfloat16)
    piece_ref[...] = jnp.broadcast_to(scaled[None], piece_ref.shape)
    picks = []
    for t in range(basis // wide):
        s = [pair[4 * t + b, row].astype(jnp.float32) for b in range(4)]
        scale = jnp.where(block == 0, s[0], jnp.where(block == 1, s[1], jnp.where(block == 2, s[2], s[3])))
        picks.append(jnp.where(hit, scale, 0.0).astype(jnp.bfloat16))
    most = send_ref.shape[0]
    step = 2
    for k in range(0, aux, step):
        for copy in copies[3 + k : 3 + k + step]:
            copy.wait()
        rows = tc[k : k + step].reshape(step * height, basis)
        for t, pick in enumerate(picks):
            cols = slice(t * LANES, (t + 1) * LANES)
            out = jnp.dot(rows[:, t * wide : (t + 1) * wide], pick, preferred_element_type=jnp.float32)
            out = out.astype(jnp.bfloat16).reshape(step, height, wide)
            keep_ref[k : k + step, :, cols] = out[:, :, :LANES]
            inside = min(step, most - k)
            send_ref[k : k + inside, :, cols] = out[:inside, :, LANES:]
            if inside < step:
                last_ref[:, :, cols] = out[inside:, :, LANES:]


def join(keep_ref, got_ref, last_ref, out_ref):
    core = lax.axis_index("core")
    aux = keep_ref.shape[0]
    most = got_ref.shape[0] // 2
    out_ref[pl.ds(core * aux, aux)] = keep_ref[...]
    out_ref[pl.ds((1 - core) * aux, most)] = got_ref[pl.ds((1 - core) * most, most)]
    out_ref[pl.ds((1 - core) * aux + most, aux - most)] = last_ref[pl.ds((1 - core) * (aux - most), aux - most)]


def pack(slab_ref, den_ref, out_ref):
    parts, height, width = slab_ref.shape
    out_ref[:, :height, :] = slab_ref[...]
    groups = width // LANES
    each = den_ref.shape[0] // groups
    for g in range(groups):
        slot = (each * g + TURN) % PLANES
        part = den_ref[slot : slot + each].reshape(each * PACK, LANES)
        spread = jnp.broadcast_to(part[None], (parts, each * PACK, LANES))
        out_ref[:, height:, g * LANES : (g + 1) * LANES] = spread


def contract(own_ref, other_ref, out_ref, den):
    core = lax.axis_index("core")
    parts, both, width = own_ref.shape
    height = both // 2
    tiles = den.shape[-1] // LANES
    groups = width // LANES
    each = den.shape[0] // groups
    for ref, side in ((own_ref, core), (other_ref, 1 - core)):
        for k in range(ROWS):
            row = (k + SHIFT) % ROWS
            cols = slice(row % tiles * LANES, (row % tiles + 1) * LANES)
            for g in range(groups):
                part = ref[k, height:, g * LANES : (g + 1) * LANES].reshape(each, PACK, LANES)
                den[each * g : each * (g + 1), side, row // tiles, :, cols] = part

    def slab(ref):
        turned = jnp.concatenate([ref[ROWS - SHIFT :, :height, :], ref[: ROWS - SHIFT, :height, :]])
        return turned.reshape(parts * height, width)

    def put(value, cols):
        value = value.astype(jnp.bfloat16).reshape(ROWS, out_ref.shape[1], width)
        out_ref[: ROWS - SHIFT, :, cols] = value[SHIFT:]
        out_ref[ROWS - SHIFT :, :, cols] = value[:SHIFT]

    own = slab(own_ref)
    density = den[...].reshape(parts * height, den.shape[-1])
    built = lax.dot_general(
        own, density, (((0,), (0,)), ((), ())), preferred_element_type=jnp.float32
    ).astype(jnp.bfloat16)
    put(jnp.dot(built, own, preferred_element_type=jnp.float32), pl.ds(pl.multiple_of(core * width, LANES), width))
    put(
        jnp.dot(built, slab(other_ref), preferred_element_type=jnp.float32),
        pl.ds(pl.multiple_of((1 - core) * width, LANES), width),
    )


def gather_groups(groups, start):
    return jnp.concatenate([g[:, start : start + HALF] for g in groups], axis=1)


def sum_aux(in_ref, out_ref):
    basis = in_ref.shape[2]
    half = basis // LANES // 2

    def total(tile):
        cols = slice(tile * LANES, (tile + 1) * LANES)
        value = in_ref[0, :, cols].astype(jnp.float32)
        for k in range(1, in_ref.shape[0]):
            value = value + in_ref[k, :, cols].astype(jnp.float32)
        return [value[8 * g : 8 * g + 8] for g in range(4)]

    for tile in range(half):
        cores = [total(tile), total(tile + half)]
        for q in range(4):
            slot = (tile * 4 + q + TURN) % PLANES
            both = jnp.concatenate([gather_groups(groups, q * HALF) for groups in cores])
            out_ref[slot * PACK : (slot + 1) * PACK, :] = both.astype(out_ref.dtype)


def sum_planes(in_ref, out_ref):
    total = in_ref[:PACK, :].astype(jnp.float32)
    for z in range(1, PLANES):
        total = total + in_ref[z * PACK : (z + 1) * PACK, :].astype(jnp.float32)
    parts = [total[8 * core : 8 * core + 8, g * HALF : (g + 1) * HALF] for core in range(2) for g in range(4)]
    out_ref[...] = jnp.concatenate(parts, axis=0).T


def body(three_centre, density, pair_mask, density_mask):
    aux, height, basis = three_centre.shape
    width = basis // 2
    bf16, f32 = jnp.bfloat16, jnp.float32
    swap = [(0, 1), (1, 0)]
    planes = PLANES
    half = jax.ShapeDtypeStruct((aux, height, width), bf16)
    most = jax.ShapeDtypeStruct((aux - 1, height, width), bf16)
    last = jax.ShapeDtypeStruct((1, height, width), bf16)
    piece, keep, send, send_last = pl.pallas_call(
        prepare,
        out_shape=(jax.ShapeDtypeStruct((planes, PACK, LANES), bf16), half, most, last),
        in_specs=[pl.BlockSpec(memory_space=pltpu.HBM)] * 4,
        out_specs=(vmem(),) * 4,
        scratch_shapes=[
            VMEM(three_centre.shape, bf16),
            VMEM((PACK, LANES), bf16),
            SMEM(pair_mask.shape, jnp.int32),
            SMEM(density_mask.shape, jnp.int32),
            pltpu.SemaphoreType.DMA((3 + aux,)),
        ],
        compiler_params=pltpu.CompilerParams(vmem_limit_bytes=40 << 20),
        name="prepare",
    )(*(pltpu.with_memory_space_constraint(a, pltpu.HBM) for a in (three_centre, density, pair_mask, density_mask)))
    turned = [(i + TURN) % PLANES for i in range(PLANES)]
    along_z = lax.all_to_all(piece, "z", 0, 0, axis_index_groups=[turned], tiled=True)
    got = lax.all_gather(send, "core", axis=0, tiled=True)
    got_last = lax.all_gather(send_last, "core", axis=0, tiled=True)
    both = pl.pallas_call(
        join,
        out_shape=jax.ShapeDtypeStruct((2 * aux, height, width), bf16),
        in_specs=[vmem()] * 3,
        out_specs=vmem(),
        compiler_params=pltpu.CompilerParams(vmem_limit_bytes=32 << 20),
        name="join",
    )(keep, got, got_last)
    slabs = pl.pallas_call(
        pack,
        out_shape=jax.ShapeDtypeStruct((2 * aux, 2 * height, width), bf16),
        in_specs=[vmem()] * 2,
        out_specs=vmem(),
        compiler_params=pltpu.CompilerParams(vmem_limit_bytes=32 << 20),
        name="pack",
    )(both, along_z)
    from_corner = [[(i + SHIFT) % ROWS for i in range(ROWS)]]
    own = lax.all_to_all(slabs, ROW, 0, 0, axis_index_groups=from_corner, tiled=True)
    other = lax.ppermute(own, "core", swap)
    partial = pl.pallas_call(
        contract,
        out_shape=jax.ShapeDtypeStruct((2 * aux, HALF, basis), bf16),
        in_specs=[vmem()] * 2,
        out_specs=vmem(),
        scratch_shapes=[VMEM((planes, 2, 2, PACK, basis), bf16)],
        compiler_params=pltpu.CompilerParams(vmem_limit_bytes=40 << 20),
        name="contract",
    )(own, other)
    pieces = lax.all_to_all(partial, ROW, 0, 0, axis_index_groups=from_corner, tiled=True)
    packed = pl.pallas_call(
        sum_aux,
        out_shape=jax.ShapeDtypeStruct((PLANES * PACK, LANES), bf16),
        in_specs=[vmem()],
        out_specs=vmem(),
        compiler_params=pltpu.CompilerParams(vmem_limit_bytes=16 << 20),
        name="sum_aux",
    )(pieces)
    pairs = [[2 * z + c for z in turned for c in range(2)]]
    arrived = lax.all_to_all(packed, COL, 0, 0, axis_index_groups=pairs, tiled=True)
    return pl.pallas_call(
        sum_planes,
        out_shape=jax.ShapeDtypeStruct((HALF, BLK), f32),
        in_specs=[vmem()],
        out_specs=vmem(),
        compiler_params=pltpu.CompilerParams(vmem_limit_bytes=16 << 20),
        name="sum_planes",
    )(arrived).T


def solution(mesh):
    fine = Mesh(mesh.devices.reshape(4, 4, 16, 2), AXES)
    return jax.shard_map(
        body,
        mesh=fine,
        in_specs=(P(COL, ROW, None), P(COL, None), P(), P()),
        out_specs=P(ROW, COL),
        check_vma=False,
    )
```

```python
import jax
import jax.numpy as jnp
from jax import lax
from jax.experimental import pallas as pl
from jax.experimental.pallas import tpu as pltpu
from jax.sharding import Mesh
from jax.sharding import PartitionSpec as P

VMEM = pltpu.VMEM
SMEM = pltpu.SMEM
AXES = ("y", "x", "z", "core")
ROW = ("y", "x")
COL = ("z", "core")
BLK = 64
HALF = 32
LANES = 128
PACK = 16
PLANES = 16
FIRST = 11
TURN = PLANES // 2
ROWS = 16
SHIFT = 10


def vmem():
    return pl.BlockSpec(memory_space=VMEM)


def smem():
    return pl.BlockSpec(memory_space=SMEM)


def prepare(
    tc_hbm, den_hbm, pair_hbm, dmask_hbm, piece_hbm, keep_ref, send_ref, last_ref, tc, den, pieces, pair, dmask, sems
):
    row = lax.axis_index("y") * 4 + lax.axis_index("x")
    core = lax.axis_index("core")
    aux, height, basis = tc.shape
    tiles = basis // LANES
    tile = row % tiles
    part = row // tiles
    piece = den_hbm.at[
        pl.ds(pl.multiple_of(part * PACK, PACK), PACK), pl.ds(pl.multiple_of(tile * LANES, LANES), LANES)
    ]
    moves = [(pair_hbm, pair), (dmask_hbm, dmask), (piece, den)]
    moves += [(tc_hbm.at[k], tc.at[k]) for k in range(aux)]
    copies = [pltpu.make_async_copy(src, dst, sems.at[k]) for k, (src, dst) in enumerate(moves)]
    for copy in copies:
        copy.start()
    wide = 2 * LANES
    src = lax.broadcasted_iota(jnp.int32, (wide, wide), 0)
    dst = lax.broadcasted_iota(jnp.int32, (wide, wide), 1)
    half = jnp.where(dst < LANES, core, 1 - core)
    lane = dst % LANES
    block = lane // HALF
    hit = src == block * BLK + half * HALF + lane % HALF
    for copy in copies[:3]:
        copy.wait()
    low = lax.broadcasted_iota(jnp.int32, (PACK, LANES), 1) < BLK
    mask_row = lax.axis_index("z")
    a = dmask[mask_row, 2 * tile].astype(jnp.float32)
    b = dmask[mask_row, 2 * tile + 1].astype(jnp.float32)
    scaled = (den[...].astype(jnp.float32) * jnp.where(low, a, b)).astype(jnp.bfloat16)
    pieces[...] = jnp.broadcast_to(scaled[None], pieces.shape)
    hand_over = pltpu.make_async_copy(pieces, piece_hbm, sems.at[3 + aux])
    hand_over.start()
    picks = []
    for t in range(basis // wide):
        s = [pair[4 * t + b, row].astype(jnp.float32) for b in range(4)]
        scale = jnp.where(block == 0, s[0], jnp.where(block == 1, s[1], jnp.where(block == 2, s[2], s[3])))
        picks.append(jnp.where(hit, scale, 0.0).astype(jnp.bfloat16))
    most = send_ref.shape[0]
    step = 2
    for k in range(0, aux, step):
        for copy in copies[3 + k : 3 + k + step]:
            copy.wait()
        rows = tc[k : k + step].reshape(step * height, basis)
        for t, pick in enumerate(picks):
            cols = slice(t * LANES, (t + 1) * LANES)
            out = jnp.dot(rows[:, t * wide : (t + 1) * wide], pick, preferred_element_type=jnp.float32)
            out = out.astype(jnp.bfloat16).reshape(step, height, wide)
            keep_ref[k : k + step, :, cols] = out[:, :, :LANES]
            inside = min(step, most - k)
            send_ref[k : k + inside, :, cols] = out[:inside, :, LANES:]
            if inside < step:
                last_ref[:, :, cols] = out[inside:, :, LANES:]
    hand_over.wait()


def join(keep_ref, got_ref, last_ref, out_ref):
    core = lax.axis_index("core")
    aux = keep_ref.shape[0]
    most = got_ref.shape[0] // 2
    out_ref[pl.ds(core * aux, aux)] = keep_ref[...]
    out_ref[pl.ds((1 - core) * aux, most)] = got_ref[pl.ds((1 - core) * most, most)]
    out_ref[pl.ds((1 - core) * aux + most, aux - most)] = last_ref[pl.ds((1 - core) * (aux - most), aux - most)]


def pack(slab_ref, den_ref, out_ref):
    parts, height, width = slab_ref.shape
    out_ref[:, :height, :] = slab_ref[...]
    groups = width // LANES
    each = PLANES // groups
    for g in range(groups):
        part = jnp.concatenate([den_ref[(z - FIRST) % PLANES] for z in range(each * g, each * (g + 1))])
        spread = jnp.broadcast_to(part[None], (parts, each * PACK, LANES))
        out_ref[:, height:, g * LANES : (g + 1) * LANES] = spread


def contract(own_ref, other_ref, out_ref, den):
    core = lax.axis_index("core")
    parts, both, width = own_ref.shape
    height = both // 2
    tiles = den.shape[-1] // LANES
    groups = width // LANES
    each = den.shape[0] // groups
    for ref, side in ((own_ref, core), (other_ref, 1 - core)):
        for k in range(ROWS):
            row = (k + SHIFT) % ROWS
            cols = slice(row % tiles * LANES, (row % tiles + 1) * LANES)
            for g in range(groups):
                part = ref[k, height:, g * LANES : (g + 1) * LANES].reshape(each, PACK, LANES)
                den[each * g : each * (g + 1), side, row // tiles, :, cols] = part

    def slab(ref):
        turned = jnp.concatenate([ref[ROWS - SHIFT :, :height, :], ref[: ROWS - SHIFT, :height, :]])
        return turned.reshape(parts * height, width)

    def put(value, cols):
        value = value.astype(jnp.bfloat16).reshape(ROWS, out_ref.shape[1], width)
        out_ref[: ROWS - SHIFT, :, cols] = value[SHIFT:]
        out_ref[ROWS - SHIFT :, :, cols] = value[:SHIFT]

    own = slab(own_ref)
    density = den[...].reshape(parts * height, den.shape[-1])
    built = lax.dot_general(
        own, density, (((0,), (0,)), ((), ())), preferred_element_type=jnp.float32
    ).astype(jnp.bfloat16)
    put(jnp.dot(built, own, preferred_element_type=jnp.float32), pl.ds(pl.multiple_of(core * width, LANES), width))
    put(
        jnp.dot(built, slab(other_ref), preferred_element_type=jnp.float32),
        pl.ds(pl.multiple_of((1 - core) * width, LANES), width),
    )


def gather_groups(groups, start):
    return jnp.concatenate([g[:, start : start + HALF] for g in groups], axis=1)


def sum_aux(in_ref, out_ref):
    basis = in_ref.shape[2]
    half = basis // LANES // 2

    def total(tile):
        cols = slice(tile * LANES, (tile + 1) * LANES)
        value = in_ref[0, :, cols].astype(jnp.float32)
        for k in range(1, in_ref.shape[0]):
            value = value + in_ref[k, :, cols].astype(jnp.float32)
        return [value[8 * g : 8 * g + 8] for g in range(4)]

    for tile in range(half):
        cores = [total(tile), total(tile + half)]
        for q in range(4):
            slot = (tile * 4 + q + TURN) % PLANES
            both = jnp.concatenate([gather_groups(groups, q * HALF) for groups in cores])
            out_ref[slot * PACK : (slot + 1) * PACK, :] = both.astype(out_ref.dtype)


def sum_planes(in_ref, out_ref):
    total = in_ref[:PACK, :].astype(jnp.float32)
    for z in range(1, PLANES):
        total = total + in_ref[z * PACK : (z + 1) * PACK, :].astype(jnp.float32)
    parts = [total[8 * core : 8 * core + 8, g * HALF : (g + 1) * HALF] for core in range(2) for g in range(4)]
    out_ref[...] = jnp.concatenate(parts, axis=0).T


def body(three_centre, density, pair_mask, density_mask):
    aux, height, basis = three_centre.shape
    width = basis // 2
    bf16, f32 = jnp.bfloat16, jnp.float32
    swap = [(0, 1), (1, 0)]
    planes = PLANES
    half = jax.ShapeDtypeStruct((aux, height, width), bf16)
    most = jax.ShapeDtypeStruct((aux - 1, height, width), bf16)
    last = jax.ShapeDtypeStruct((1, height, width), bf16)
    piece, keep, send, send_last = pl.pallas_call(
        prepare,
        out_shape=(jax.ShapeDtypeStruct((planes, PACK, LANES), bf16), half, most, last),
        in_specs=[pl.BlockSpec(memory_space=pltpu.HBM)] * 4,
        out_specs=(pl.BlockSpec(memory_space=pltpu.HBM), vmem(), vmem(), vmem()),
        scratch_shapes=[
            VMEM(three_centre.shape, bf16),
            VMEM((PACK, LANES), bf16),
            VMEM((planes, PACK, LANES), bf16),
            SMEM(pair_mask.shape, jnp.int32),
            SMEM(density_mask.shape, jnp.int32),
            pltpu.SemaphoreType.DMA((4 + aux,)),
        ],
        compiler_params=pltpu.CompilerParams(vmem_limit_bytes=40 << 20),
        name="prepare",
    )(*(pltpu.with_memory_space_constraint(a, pltpu.HBM) for a in (three_centre, density, pair_mask, density_mask)))
    late_first = [(i + FIRST) % PLANES for i in range(PLANES)]
    along_z = lax.all_to_all(piece, "z", 0, 0, axis_index_groups=[late_first], tiled=True)
    got = lax.all_gather(send, "core", axis=0, tiled=True)
    got_last = lax.all_gather(send_last, "core", axis=0, tiled=True)
    both = pl.pallas_call(
        join,
        out_shape=jax.ShapeDtypeStruct((2 * aux, height, width), bf16),
        in_specs=[vmem()] * 3,
        out_specs=vmem(),
        compiler_params=pltpu.CompilerParams(vmem_limit_bytes=32 << 20),
        name="join",
    )(keep, got, got_last)
    slabs = pl.pallas_call(
        pack,
        out_shape=jax.ShapeDtypeStruct((2 * aux, 2 * height, width), bf16),
        in_specs=[vmem()] * 2,
        out_specs=vmem(),
        compiler_params=pltpu.CompilerParams(vmem_limit_bytes=32 << 20),
        name="pack",
    )(both, along_z)
    from_corner = [[(i + SHIFT) % ROWS for i in range(ROWS)]]
    own = lax.all_to_all(slabs, ROW, 0, 0, axis_index_groups=from_corner, tiled=True)
    other = lax.ppermute(own, "core", swap)
    partial = pl.pallas_call(
        contract,
        out_shape=jax.ShapeDtypeStruct((2 * aux, HALF, basis), bf16),
        in_specs=[vmem()] * 2,
        out_specs=vmem(),
        scratch_shapes=[VMEM((planes, 2, 2, PACK, basis), bf16)],
        compiler_params=pltpu.CompilerParams(vmem_limit_bytes=40 << 20),
        name="contract",
    )(own, other)
    pieces = lax.all_to_all(partial, ROW, 0, 0, axis_index_groups=from_corner, tiled=True)
    packed = pl.pallas_call(
        sum_aux,
        out_shape=jax.ShapeDtypeStruct((PLANES * PACK, LANES), bf16),
        in_specs=[vmem()],
        out_specs=vmem(),
        compiler_params=pltpu.CompilerParams(vmem_limit_bytes=16 << 20),
        name="sum_aux",
    )(pieces)
    turned = [(i + TURN) % PLANES for i in range(PLANES)]
    pairs = [[2 * z + c for z in turned for c in range(2)]]
    arrived = lax.all_to_all(packed, COL, 0, 0, axis_index_groups=pairs, tiled=True)
    return pl.pallas_call(
        sum_planes,
        out_shape=jax.ShapeDtypeStruct((HALF, BLK), f32),
        in_specs=[vmem()],
        out_specs=vmem(),
        compiler_params=pltpu.CompilerParams(vmem_limit_bytes=16 << 20),
        name="sum_planes",
    )(arrived).T


def solution(mesh):
    fine = Mesh(mesh.devices.reshape(4, 4, 16, 2), AXES)
    return jax.shard_map(
        body,
        mesh=fine,
        in_specs=(P(COL, ROW, None), P(COL, None), P(), P()),
        out_specs=P(ROW, COL),
        check_vma=False,
    )
```

```python
import jax
import jax.numpy as jnp
from jax import lax
from jax.experimental import pallas as pl
from jax.experimental.pallas import tpu as pltpu
from jax.sharding import Mesh
from jax.sharding import PartitionSpec as P

VMEM = pltpu.VMEM
SMEM = pltpu.SMEM
AXES = ("y", "x", "z", "core")
ROW = ("y", "x")
COL = ("z", "core")
BLK = 64
HALF = 32
LANES = 128
PACK = 16
PLANES = 16
FIRST = 11
TURN = PLANES // 2
ROWS = 16
SHIFT = 10


def vmem():
    return pl.BlockSpec(memory_space=VMEM)


def smem():
    return pl.BlockSpec(memory_space=SMEM)


def prepare(
    tc_hbm, den_hbm, pair_hbm, dmask_hbm, piece_hbm, keep_ref, send_ref, last_ref, tc, den, pieces, pair, dmask, sems
):
    row = lax.axis_index("y") * 4 + lax.axis_index("x")
    core = lax.axis_index("core")
    aux, height, basis = tc.shape
    tiles = basis // LANES
    tile = row % tiles
    part = row // tiles
    piece = den_hbm.at[
        pl.ds(pl.multiple_of(part * PACK, PACK), PACK), pl.ds(pl.multiple_of(tile * LANES, LANES), LANES)
    ]
    moves = [(pair_hbm, pair), (dmask_hbm, dmask), (piece, den)]
    moves += [(tc_hbm.at[k], tc.at[k]) for k in range(aux)]
    copies = [pltpu.make_async_copy(src, dst, sems.at[k]) for k, (src, dst) in enumerate(moves)]
    for copy in copies:
        copy.start()
    wide = 2 * LANES
    src = lax.broadcasted_iota(jnp.int32, (wide, wide), 0)
    dst = lax.broadcasted_iota(jnp.int32, (wide, wide), 1)
    half = jnp.where(dst < LANES, core, 1 - core)
    lane = dst % LANES
    block = lane // HALF
    hit = src == block * BLK + half * HALF + lane % HALF
    for copy in copies[:3]:
        copy.wait()
    low = lax.broadcasted_iota(jnp.int32, (PACK, LANES), 1) < BLK
    mask_row = lax.axis_index("z")
    a = dmask[mask_row, 2 * tile].astype(jnp.float32)
    b = dmask[mask_row, 2 * tile + 1].astype(jnp.float32)
    scaled = (den[...].astype(jnp.float32) * jnp.where(low, a, b)).astype(jnp.bfloat16)
    pieces[...] = jnp.broadcast_to(scaled[None], pieces.shape)
    hand_over = pltpu.make_async_copy(pieces, piece_hbm, sems.at[3 + aux])
    hand_over.start()
    picks = []
    for t in range(basis // wide):
        s = [pair[4 * t + b, row].astype(jnp.float32) for b in range(4)]
        scale = jnp.where(block == 0, s[0], jnp.where(block == 1, s[1], jnp.where(block == 2, s[2], s[3])))
        picks.append(jnp.where(hit, scale, 0.0).astype(jnp.bfloat16))
    most = send_ref.shape[0]
    step = 2
    for k in range(0, aux, step):
        for copy in copies[3 + k : 3 + k + step]:
            copy.wait()
        rows = tc[k : k + step].reshape(step * height, basis)
        for t, pick in enumerate(picks):
            cols = slice(t * LANES, (t + 1) * LANES)
            out = jnp.dot(rows[:, t * wide : (t + 1) * wide], pick, preferred_element_type=jnp.float32)
            out = out.astype(jnp.bfloat16).reshape(step, height, wide)
            keep_ref[k : k + step, :, cols] = out[:, :, :LANES]
            inside = min(step, most - k)
            send_ref[k : k + inside, :, cols] = out[:inside, :, LANES:]
            if inside < step:
                last_ref[:, :, cols] = out[inside:, :, LANES:]
    hand_over.wait()


def join(keep_ref, got_ref, last_ref, out_ref):
    core = lax.axis_index("core")
    aux = keep_ref.shape[0]
    most = got_ref.shape[0] // 2
    out_ref[pl.ds(core * aux, aux)] = keep_ref[...]
    out_ref[pl.ds((1 - core) * aux, most)] = got_ref[pl.ds((1 - core) * most, most)]
    out_ref[pl.ds((1 - core) * aux + most, aux - most)] = last_ref[pl.ds((1 - core) * (aux - most), aux - most)]


def pack(slab_ref, den_ref, out_ref):
    parts, height, width = slab_ref.shape
    out_ref[:, :height, :] = slab_ref[...]
    groups = width // LANES
    each = PLANES // groups
    for g in range(groups):
        part = jnp.concatenate([den_ref[(z - FIRST) % PLANES] for z in range(each * g, each * (g + 1))])
        spread = jnp.broadcast_to(part[None], (parts, each * PACK, LANES))
        out_ref[:, height:, g * LANES : (g + 1) * LANES] = spread


def place(ref, den):
    height = ref.shape[1] // 2
    tiles = den.shape[-1] // LANES
    groups = ref.shape[2] // LANES
    each = PLANES // groups
    for k in range(ROWS):
        row = (k + SHIFT) % ROWS
        cols = slice(row % tiles * LANES, (row % tiles + 1) * LANES)
        for g in range(groups):
            part = ref[k, height:, g * LANES : (g + 1) * LANES].reshape(each, PACK, LANES)
            den[each * g : each * (g + 1), row // tiles, :, cols] = part


def slab_rows(ref, start, count):
    rows = pl.ds(start, count)
    turned = jnp.concatenate([ref[ROWS - SHIFT :, rows, :], ref[: ROWS - SHIFT, rows, :]])
    return turned.reshape(ROWS * count, ref.shape[2])


def half_sum(ref, own_ref, side, den):
    place(ref, den)
    own = slab_rows(own_ref, pl.multiple_of(side * HALF, HALF), HALF)
    density = den[...].reshape(ROWS * HALF, den.shape[-1])
    return lax.dot_general(own, density, (((0,), (0,)), ((), ())), preferred_element_type=jnp.float32)


def begin(own_ref, sum_ref, den):
    sum_ref[...] = half_sum(own_ref, own_ref, lax.axis_index("core"), den)


def contract(own_ref, other_ref, sum_ref, out_ref, den):
    core = lax.axis_index("core")
    width = own_ref.shape[2]

    def put(value, cols):
        value = value.astype(jnp.bfloat16).reshape(ROWS, out_ref.shape[1], width)
        out_ref[: ROWS - SHIFT, :, cols] = value[SHIFT:]
        out_ref[ROWS - SHIFT :, :, cols] = value[:SHIFT]

    built = (sum_ref[...] + half_sum(other_ref, own_ref, 1 - core, den)).astype(jnp.bfloat16)
    own = slab_rows(own_ref, 0, BLK)
    put(jnp.dot(built, own, preferred_element_type=jnp.float32), pl.ds(pl.multiple_of(core * width, LANES), width))
    put(
        jnp.dot(built, slab_rows(other_ref, 0, BLK), preferred_element_type=jnp.float32),
        pl.ds(pl.multiple_of((1 - core) * width, LANES), width),
    )


def gather_groups(groups, start):
    return jnp.concatenate([g[:, start : start + HALF] for g in groups], axis=1)


def sum_aux(in_ref, out_ref):
    basis = in_ref.shape[2]
    half = basis // LANES // 2

    def total(tile):
        cols = slice(tile * LANES, (tile + 1) * LANES)
        value = in_ref[0, :, cols].astype(jnp.float32)
        for k in range(1, in_ref.shape[0]):
            value = value + in_ref[k, :, cols].astype(jnp.float32)
        return [value[8 * g : 8 * g + 8] for g in range(4)]

    for tile in range(half):
        cores = [total(tile), total(tile + half)]
        for q in range(4):
            slot = (tile * 4 + q + TURN) % PLANES
            both = jnp.concatenate([gather_groups(groups, q * HALF) for groups in cores])
            out_ref[slot * PACK : (slot + 1) * PACK, :] = both.astype(out_ref.dtype)


def sum_planes(in_ref, out_ref):
    total = in_ref[:PACK, :].astype(jnp.float32)
    for z in range(1, PLANES):
        total = total + in_ref[z * PACK : (z + 1) * PACK, :].astype(jnp.float32)
    parts = [total[8 * core : 8 * core + 8, g * HALF : (g + 1) * HALF] for core in range(2) for g in range(4)]
    out_ref[...] = jnp.concatenate(parts, axis=0).T


def body(three_centre, density, pair_mask, density_mask):
    aux, height, basis = three_centre.shape
    width = basis // 2
    bf16, f32 = jnp.bfloat16, jnp.float32
    swap = [(0, 1), (1, 0)]
    planes = PLANES
    half = jax.ShapeDtypeStruct((aux, height, width), bf16)
    most = jax.ShapeDtypeStruct((aux - 1, height, width), bf16)
    last = jax.ShapeDtypeStruct((1, height, width), bf16)
    piece, keep, send, send_last = pl.pallas_call(
        prepare,
        out_shape=(jax.ShapeDtypeStruct((planes, PACK, LANES), bf16), half, most, last),
        in_specs=[pl.BlockSpec(memory_space=pltpu.HBM)] * 4,
        out_specs=(pl.BlockSpec(memory_space=pltpu.HBM), vmem(), vmem(), vmem()),
        scratch_shapes=[
            VMEM(three_centre.shape, bf16),
            VMEM((PACK, LANES), bf16),
            VMEM((planes, PACK, LANES), bf16),
            SMEM(pair_mask.shape, jnp.int32),
            SMEM(density_mask.shape, jnp.int32),
            pltpu.SemaphoreType.DMA((4 + aux,)),
        ],
        compiler_params=pltpu.CompilerParams(vmem_limit_bytes=40 << 20),
        name="prepare",
    )(*(pltpu.with_memory_space_constraint(a, pltpu.HBM) for a in (three_centre, density, pair_mask, density_mask)))
    late_first = [(i + FIRST) % PLANES for i in range(PLANES)]
    along_z = lax.all_to_all(piece, "z", 0, 0, axis_index_groups=[late_first], tiled=True)
    got = lax.all_gather(send, "core", axis=0, tiled=True)
    got_last = lax.all_gather(send_last, "core", axis=0, tiled=True)
    both = pl.pallas_call(
        join,
        out_shape=jax.ShapeDtypeStruct((2 * aux, height, width), bf16),
        in_specs=[vmem()] * 3,
        out_specs=vmem(),
        compiler_params=pltpu.CompilerParams(vmem_limit_bytes=32 << 20),
        name="join",
    )(keep, got, got_last)
    slabs = pl.pallas_call(
        pack,
        out_shape=jax.ShapeDtypeStruct((2 * aux, 2 * height, width), bf16),
        in_specs=[vmem()] * 2,
        out_specs=vmem(),
        compiler_params=pltpu.CompilerParams(vmem_limit_bytes=32 << 20),
        name="pack",
    )(both, along_z)
    from_corner = [[(i + SHIFT) % ROWS for i in range(ROWS)]]
    own = lax.all_to_all(slabs, ROW, 0, 0, axis_index_groups=from_corner, tiled=True)
    other = lax.ppermute(own, "core", swap)
    den_scratch = VMEM((planes, 2, PACK, basis), bf16)
    own_sum = pl.pallas_call(
        begin,
        out_shape=jax.ShapeDtypeStruct((width, basis), f32),
        in_specs=[vmem()],
        out_specs=vmem(),
        scratch_shapes=[den_scratch],
        compiler_params=pltpu.CompilerParams(vmem_limit_bytes=32 << 20),
        cost_estimate=pl.CostEstimate(flops=width * width * basis * 2, bytes_accessed=4 << 20, transcendentals=0),
        name="begin",
    )(own)
    partial = pl.pallas_call(
        contract,
        out_shape=jax.ShapeDtypeStruct((2 * aux, HALF, basis), bf16),
        in_specs=[vmem()] * 3,
        out_specs=vmem(),
        scratch_shapes=[den_scratch],
        compiler_params=pltpu.CompilerParams(vmem_limit_bytes=40 << 20),
        name="contract",
    )(own, other, own_sum)
    pieces = lax.all_to_all(partial, ROW, 0, 0, axis_index_groups=from_corner, tiled=True)
    packed = pl.pallas_call(
        sum_aux,
        out_shape=jax.ShapeDtypeStruct((PLANES * PACK, LANES), bf16),
        in_specs=[vmem()],
        out_specs=vmem(),
        compiler_params=pltpu.CompilerParams(vmem_limit_bytes=16 << 20),
        name="sum_aux",
    )(pieces)
    turned = [(i + TURN) % PLANES for i in range(PLANES)]
    pairs = [[2 * z + c for z in turned for c in range(2)]]
    arrived = lax.all_to_all(packed, COL, 0, 0, axis_index_groups=pairs, tiled=True)
    return pl.pallas_call(
        sum_planes,
        out_shape=jax.ShapeDtypeStruct((HALF, BLK), f32),
        in_specs=[vmem()],
        out_specs=vmem(),
        compiler_params=pltpu.CompilerParams(vmem_limit_bytes=16 << 20),
        name="sum_planes",
    )(arrived).T


def solution(mesh):
    fine = Mesh(mesh.devices.reshape(4, 4, 16, 2), AXES)
    return jax.shard_map(
        body,
        mesh=fine,
        in_specs=(P(COL, ROW, None), P(COL, None), P(), P()),
        out_specs=P(ROW, COL),
        check_vma=False,
    )
```

```python
import jax
import jax.numpy as jnp
from jax import lax
from jax.experimental import pallas as pl
from jax.experimental.pallas import tpu as pltpu
from jax.sharding import Mesh
from jax.sharding import PartitionSpec as P

VMEM = pltpu.VMEM
SMEM = pltpu.SMEM
AXES = ("y", "x", "z", "core")
ROW = ("y", "x")
COL = ("z", "core")
BLK = 64
HALF = 32
LANES = 128
PACK = 16
PLANES = 16
FIRST = 11
TURN = 9
ROWS = 16
SHIFT = 10


def vmem():
    return pl.BlockSpec(memory_space=VMEM)


def smem():
    return pl.BlockSpec(memory_space=SMEM)


def prepare(
    tc_hbm, den_hbm, pair_hbm, dmask_hbm, piece_hbm, keep_ref, send_ref, last_ref, tc, den, pieces, pair, dmask, sems
):
    row = lax.axis_index("y") * 4 + lax.axis_index("x")
    core = lax.axis_index("core")
    aux, height, basis = tc.shape
    tiles = basis // LANES
    tile = row % tiles
    part = row // tiles
    piece = den_hbm.at[
        pl.ds(pl.multiple_of(part * PACK, PACK), PACK), pl.ds(pl.multiple_of(tile * LANES, LANES), LANES)
    ]
    moves = [(pair_hbm, pair), (dmask_hbm, dmask), (piece, den)]
    moves += [(tc_hbm.at[k], tc.at[k]) for k in range(aux)]
    copies = [pltpu.make_async_copy(src, dst, sems.at[k]) for k, (src, dst) in enumerate(moves)]
    for copy in copies:
        copy.start()
    wide = 2 * LANES
    src = lax.broadcasted_iota(jnp.int32, (wide, wide), 0)
    dst = lax.broadcasted_iota(jnp.int32, (wide, wide), 1)
    half = jnp.where(dst < LANES, core, 1 - core)
    lane = dst % LANES
    block = lane // HALF
    hit = src == block * BLK + half * HALF + lane % HALF
    for copy in copies[:3]:
        copy.wait()
    low = lax.broadcasted_iota(jnp.int32, (PACK, LANES), 1) < BLK
    mask_row = lax.axis_index("z")
    a = dmask[mask_row, 2 * tile].astype(jnp.float32)
    b = dmask[mask_row, 2 * tile + 1].astype(jnp.float32)
    scaled = (den[...].astype(jnp.float32) * jnp.where(low, a, b)).astype(jnp.bfloat16)
    pieces[...] = jnp.broadcast_to(scaled[None], pieces.shape)
    hand_over = pltpu.make_async_copy(pieces, piece_hbm, sems.at[3 + aux])
    hand_over.start()
    picks = []
    for t in range(basis // wide):
        s = [pair[4 * t + b, row].astype(jnp.float32) for b in range(4)]
        scale = jnp.where(block == 0, s[0], jnp.where(block == 1, s[1], jnp.where(block == 2, s[2], s[3])))
        picks.append(jnp.where(hit, scale, 0.0).astype(jnp.bfloat16))
    most = send_ref.shape[0]
    step = 4
    for k in range(0, aux, step):
        for copy in copies[3 + k : 3 + k + step]:
            copy.wait()
        rows = tc[k : k + step].reshape(step * height, basis)
        for t, pick in enumerate(picks):
            cols = slice(t * LANES, (t + 1) * LANES)
            out = jnp.dot(rows[:, t * wide : (t + 1) * wide], pick, preferred_element_type=jnp.float32)
            out = out.astype(jnp.bfloat16).reshape(step, height, wide)
            keep_ref[k : k + step, :, cols] = out[:, :, :LANES]
            inside = min(step, most - k)
            send_ref[k : k + inside, :, cols] = out[:inside, :, LANES:]
            if inside < step:
                last_ref[:, :, cols] = out[inside:, :, LANES:]
    hand_over.wait()


def join(keep_ref, got_ref, last_ref, out_ref):
    core = lax.axis_index("core")
    aux = keep_ref.shape[0]
    most = got_ref.shape[0] // 2
    out_ref[pl.ds(core * aux, aux)] = keep_ref[...]
    out_ref[pl.ds((1 - core) * aux, most)] = got_ref[pl.ds((1 - core) * most, most)]
    out_ref[pl.ds((1 - core) * aux + most, aux - most)] = last_ref[pl.ds((1 - core) * (aux - most), aux - most)]


def pack(slab_ref, den_ref, out_ref):
    parts, height, width = slab_ref.shape
    out_ref[:, :height, :] = slab_ref[...]
    groups = width // LANES
    each = PLANES // groups
    for g in range(groups):
        part = jnp.concatenate([den_ref[(z - FIRST) % PLANES] for z in range(each * g, each * (g + 1))])
        spread = jnp.broadcast_to(part[None], (parts, each * PACK, LANES))
        out_ref[:, height:, g * LANES : (g + 1) * LANES] = spread


def place(ref, den):
    height = ref.shape[1] // 2
    tiles = den.shape[-1] // LANES
    groups = ref.shape[2] // LANES
    each = PLANES // groups
    for k in range(ROWS):
        row = (k + SHIFT) % ROWS
        cols = slice(row % tiles * LANES, (row % tiles + 1) * LANES)
        for g in range(groups):
            part = ref[k, height:, g * LANES : (g + 1) * LANES].reshape(each, PACK, LANES)
            den[each * g : each * (g + 1), row // tiles, :, cols] = part


def slab_rows(ref, start, count):
    rows = pl.ds(start, count)
    turned = jnp.concatenate([ref[ROWS - SHIFT :, rows, :], ref[: ROWS - SHIFT, rows, :]])
    return turned.reshape(ROWS * count, ref.shape[2])


def half_sum(ref, own_ref, side, den):
    place(ref, den)
    own = slab_rows(own_ref, pl.multiple_of(side * HALF, HALF), HALF)
    density = den[...].reshape(ROWS * HALF, den.shape[-1])
    return lax.dot_general(own, density, (((0,), (0,)), ((), ())), preferred_element_type=jnp.float32)


def begin(own_ref, sum_ref, den):
    sum_ref[...] = half_sum(own_ref, own_ref, lax.axis_index("core"), den)


def contract(own_ref, other_ref, sum_ref, out_ref, den):
    core = lax.axis_index("core")
    width = own_ref.shape[2]

    def put(value, cols):
        value = value.astype(jnp.bfloat16).reshape(ROWS, out_ref.shape[1], width)
        out_ref[: ROWS - SHIFT, :, cols] = value[SHIFT:]
        out_ref[ROWS - SHIFT :, :, cols] = value[:SHIFT]

    built = (sum_ref[...] + half_sum(other_ref, own_ref, 1 - core, den)).astype(jnp.bfloat16)
    own = slab_rows(own_ref, 0, BLK)
    put(jnp.dot(built, own, preferred_element_type=jnp.float32), pl.ds(pl.multiple_of(core * width, LANES), width))
    put(
        jnp.dot(built, slab_rows(other_ref, 0, BLK), preferred_element_type=jnp.float32),
        pl.ds(pl.multiple_of((1 - core) * width, LANES), width),
    )


def gather_groups(groups, start):
    return jnp.concatenate([g[:, start : start + HALF] for g in groups], axis=1)


def sum_aux(in_ref, out_ref):
    basis = in_ref.shape[2]
    half = basis // LANES // 2

    def total(tile):
        cols = slice(tile * LANES, (tile + 1) * LANES)
        value = in_ref[0, :, cols].astype(jnp.float32)
        for k in range(1, in_ref.shape[0]):
            value = value + in_ref[k, :, cols].astype(jnp.float32)
        return [value[8 * g : 8 * g + 8] for g in range(4)]

    for tile in range(half):
        cores = [total(tile), total(tile + half)]
        for q in range(4):
            slot = (tile * 4 + q - TURN) % PLANES
            both = jnp.concatenate([gather_groups(groups, q * HALF) for groups in cores])
            out_ref[slot * PACK : (slot + 1) * PACK, :] = both.astype(out_ref.dtype)


def sum_planes(in_ref, out_ref):
    total = in_ref[:PACK, :].astype(jnp.float32)
    for z in range(1, PLANES):
        total = total + in_ref[z * PACK : (z + 1) * PACK, :].astype(jnp.float32)
    parts = [total[8 * core : 8 * core + 8, g * HALF : (g + 1) * HALF] for core in range(2) for g in range(4)]
    out_ref[...] = jnp.concatenate(parts, axis=0).T


def body(three_centre, density, pair_mask, density_mask):
    aux, height, basis = three_centre.shape
    width = basis // 2
    bf16, f32 = jnp.bfloat16, jnp.float32
    swap = [(0, 1), (1, 0)]
    planes = PLANES
    half = jax.ShapeDtypeStruct((aux, height, width), bf16)
    most = jax.ShapeDtypeStruct((aux - 1, height, width), bf16)
    last = jax.ShapeDtypeStruct((1, height, width), bf16)
    piece, keep, send, send_last = pl.pallas_call(
        prepare,
        out_shape=(jax.ShapeDtypeStruct((planes, PACK, LANES), bf16), half, most, last),
        in_specs=[pl.BlockSpec(memory_space=pltpu.HBM)] * 4,
        out_specs=(pl.BlockSpec(memory_space=pltpu.HBM), vmem(), vmem(), vmem()),
        scratch_shapes=[
            VMEM(three_centre.shape, bf16),
            VMEM((PACK, LANES), bf16),
            VMEM((planes, PACK, LANES), bf16),
            SMEM(pair_mask.shape, jnp.int32),
            SMEM(density_mask.shape, jnp.int32),
            pltpu.SemaphoreType.DMA((4 + aux,)),
        ],
        compiler_params=pltpu.CompilerParams(vmem_limit_bytes=40 << 20),
        name="prepare",
    )(*(pltpu.with_memory_space_constraint(a, pltpu.HBM) for a in (three_centre, density, pair_mask, density_mask)))
    late_first = [(i + FIRST) % PLANES for i in range(PLANES)]
    along_z = lax.all_to_all(piece, "z", 0, 0, axis_index_groups=[late_first], tiled=True)
    got = lax.all_gather(send, "core", axis=0, tiled=True)
    got_last = lax.all_gather(send_last, "core", axis=0, tiled=True)
    both = pl.pallas_call(
        join,
        out_shape=jax.ShapeDtypeStruct((2 * aux, height, width), bf16),
        in_specs=[vmem()] * 3,
        out_specs=vmem(),
        compiler_params=pltpu.CompilerParams(vmem_limit_bytes=32 << 20),
        name="join",
    )(keep, got, got_last)
    slabs = pl.pallas_call(
        pack,
        out_shape=jax.ShapeDtypeStruct((2 * aux, 2 * height, width), bf16),
        in_specs=[vmem()] * 2,
        out_specs=vmem(),
        compiler_params=pltpu.CompilerParams(vmem_limit_bytes=32 << 20),
        name="pack",
    )(both, along_z)
    from_corner = [[(i + SHIFT) % ROWS for i in range(ROWS)]]
    own = lax.all_to_all(slabs, ROW, 0, 0, axis_index_groups=from_corner, tiled=True)
    other = lax.ppermute(own, "core", swap)
    den_scratch = VMEM((planes, 2, PACK, basis), bf16)
    own_sum = pl.pallas_call(
        begin,
        out_shape=jax.ShapeDtypeStruct((width, basis), f32),
        in_specs=[vmem()],
        out_specs=vmem(),
        scratch_shapes=[den_scratch],
        compiler_params=pltpu.CompilerParams(vmem_limit_bytes=32 << 20),
        cost_estimate=pl.CostEstimate(flops=width * width * basis * 2, bytes_accessed=4 << 20, transcendentals=0),
        name="begin",
    )(own)
    partial = pl.pallas_call(
        contract,
        out_shape=jax.ShapeDtypeStruct((2 * aux, HALF, basis), bf16),
        in_specs=[vmem()] * 3,
        out_specs=vmem(),
        scratch_shapes=[den_scratch],
        compiler_params=pltpu.CompilerParams(vmem_limit_bytes=40 << 20),
        name="contract",
    )(own, other, own_sum)
    pieces = lax.all_to_all(partial, ROW, 0, 0, axis_index_groups=from_corner, tiled=True)
    packed = pl.pallas_call(
        sum_aux,
        out_shape=jax.ShapeDtypeStruct((PLANES * PACK, LANES), bf16),
        in_specs=[vmem()],
        out_specs=vmem(),
        compiler_params=pltpu.CompilerParams(vmem_limit_bytes=16 << 20),
        name="sum_aux",
    )(pieces)
    turned = [(i + TURN) % PLANES for i in range(PLANES)]
    pairs = [[2 * z + c for z in turned for c in range(2)]]
    arrived = lax.all_to_all(packed, COL, 0, 0, axis_index_groups=pairs, tiled=True)
    return pl.pallas_call(
        sum_planes,
        out_shape=jax.ShapeDtypeStruct((HALF, BLK), f32),
        in_specs=[vmem()],
        out_specs=vmem(),
        compiler_params=pltpu.CompilerParams(vmem_limit_bytes=16 << 20),
        name="sum_planes",
    )(arrived).T


def solution(mesh):
    fine = Mesh(mesh.devices.reshape(4, 4, 16, 2), AXES)
    return jax.shard_map(
        body,
        mesh=fine,
        in_specs=(P(COL, ROW, None), P(COL, None), P(), P()),
        out_specs=P(ROW, COL),
        check_vma=False,
    )
```

```python
import jax
import jax.numpy as jnp
from jax import lax
from jax.experimental import pallas as pl
from jax.experimental.pallas import tpu as pltpu
from jax.sharding import Mesh
from jax.sharding import PartitionSpec as P

VMEM = pltpu.VMEM
SMEM = pltpu.SMEM
AXES = ("y", "x", "z", "core")
ROW = ("y", "x")
COL = ("z", "core")
BLK = 64
HALF = 32
LANES = 128
PACK = 16
PLANES = 16
FIRST = 10
TURN = 9
ROWS = 16
SHIFT = 10


def vmem():
    return pl.BlockSpec(memory_space=VMEM)


def smem():
    return pl.BlockSpec(memory_space=SMEM)


def prepare(
    tc_hbm, den_hbm, pair_hbm, dmask_hbm, piece_hbm, keep_ref, send_ref, last_ref, tc, den, pieces, pair, dmask, sems
):
    row = lax.axis_index("y") * 4 + lax.axis_index("x")
    core = lax.axis_index("core")
    aux, height, basis = tc.shape
    tiles = basis // LANES
    tile = row % tiles
    part = row // tiles
    piece = den_hbm.at[
        pl.ds(pl.multiple_of(part * PACK, PACK), PACK), pl.ds(pl.multiple_of(tile * LANES, LANES), LANES)
    ]
    moves = [(pair_hbm, pair), (dmask_hbm, dmask), (piece, den)]
    moves += [(tc_hbm.at[k], tc.at[k]) for k in range(aux)]
    copies = [pltpu.make_async_copy(src, dst, sems.at[k]) for k, (src, dst) in enumerate(moves)]
    for copy in copies:
        copy.start()
    wide = 2 * LANES
    src = lax.broadcasted_iota(jnp.int32, (wide, wide), 0)
    dst = lax.broadcasted_iota(jnp.int32, (wide, wide), 1)
    half = jnp.where(dst < LANES, core, 1 - core)
    lane = dst % LANES
    block = lane // HALF
    hit = src == block * BLK + half * HALF + lane % HALF
    for copy in copies[:3]:
        copy.wait()
    low = lax.broadcasted_iota(jnp.int32, (PACK, LANES), 1) < BLK
    mask_row = lax.axis_index("z")
    a = dmask[mask_row, 2 * tile].astype(jnp.float32)
    b = dmask[mask_row, 2 * tile + 1].astype(jnp.float32)
    scaled = (den[...].astype(jnp.float32) * jnp.where(low, a, b)).astype(jnp.bfloat16)
    pieces[...] = jnp.broadcast_to(scaled[None], pieces.shape)
    hand_over = pltpu.make_async_copy(pieces, piece_hbm, sems.at[3 + aux])
    hand_over.start()
    picks = []
    for t in range(basis // wide):
        s = [pair[4 * t + b, row].astype(jnp.float32) for b in range(4)]
        scale = jnp.where(block == 0, s[0], jnp.where(block == 1, s[1], jnp.where(block == 2, s[2], s[3])))
        picks.append(jnp.where(hit, scale, 0.0).astype(jnp.bfloat16))
    most = send_ref.shape[0]
    step = 4
    for k in range(0, aux, step):
        for copy in copies[3 + k : 3 + k + step]:
            copy.wait()
        rows = tc[k : k + step].reshape(step * height, basis)
        for t, pick in enumerate(picks):
            cols = slice(t * LANES, (t + 1) * LANES)
            out = jnp.dot(rows[:, t * wide : (t + 1) * wide], pick, preferred_element_type=jnp.float32)
            out = out.astype(jnp.bfloat16).reshape(step, height, wide)
            keep_ref[k : k + step, :, cols] = out[:, :, :LANES]
            inside = min(step, most - k)
            send_ref[k : k + inside, :, cols] = out[:inside, :, LANES:]
            if inside < step:
                last_ref[:, :, cols] = out[inside:, :, LANES:]
    hand_over.wait()


def join(keep_ref, got_ref, last_ref, out_ref):
    core = lax.axis_index("core")
    aux = keep_ref.shape[0]
    most = got_ref.shape[0] // 2
    out_ref[pl.ds(core * aux, aux)] = keep_ref[...]
    out_ref[pl.ds((1 - core) * aux, most)] = got_ref[pl.ds((1 - core) * most, most)]
    out_ref[pl.ds((1 - core) * aux + most, aux - most)] = last_ref[pl.ds((1 - core) * (aux - most), aux - most)]


def pack(slab_ref, den_ref, out_ref):
    parts, height, width = slab_ref.shape
    out_ref[:, :height, :] = slab_ref[...]
    groups = width // LANES
    each = PLANES // groups
    for g in range(groups):
        part = jnp.concatenate([den_ref[(z - FIRST) % PLANES] for z in range(each * g, each * (g + 1))])
        spread = jnp.broadcast_to(part[None], (parts, each * PACK, LANES))
        out_ref[:, height:, g * LANES : (g + 1) * LANES] = spread


def place(ref, den):
    height = ref.shape[1] // 2
    tiles = den.shape[-1] // LANES
    groups = ref.shape[2] // LANES
    each = PLANES // groups
    for k in range(ROWS):
        row = (k + SHIFT) % ROWS
        cols = slice(row % tiles * LANES, (row % tiles + 1) * LANES)
        for g in range(groups):
            part = ref[k, height:, g * LANES : (g + 1) * LANES].reshape(each, PACK, LANES)
            den[each * g : each * (g + 1), row // tiles, :, cols] = part


def slab_rows(ref, start, count):
    rows = pl.ds(start, count)
    turned = jnp.concatenate([ref[ROWS - SHIFT :, rows, :], ref[: ROWS - SHIFT, rows, :]])
    return turned.reshape(ROWS * count, ref.shape[2])


def half_sum(ref, own_ref, side, den):
    place(ref, den)
    own = slab_rows(own_ref, pl.multiple_of(side * HALF, HALF), HALF)
    density = den[...].reshape(ROWS * HALF, den.shape[-1])
    return lax.dot_general(own, density, (((0,), (0,)), ((), ())), preferred_element_type=jnp.float32)


def begin(own_ref, sum_ref, den):
    sum_ref[...] = half_sum(own_ref, own_ref, lax.axis_index("core"), den)


def contract(own_ref, other_ref, sum_ref, out_ref, den):
    core = lax.axis_index("core")
    width = own_ref.shape[2]

    def put(value, cols):
        value = value.astype(jnp.bfloat16).reshape(ROWS, out_ref.shape[1], width)
        out_ref[: ROWS - SHIFT, :, cols] = value[SHIFT:]
        out_ref[ROWS - SHIFT :, :, cols] = value[:SHIFT]

    built = (sum_ref[...] + half_sum(other_ref, own_ref, 1 - core, den)).astype(jnp.bfloat16)
    own = slab_rows(own_ref, 0, BLK)
    put(jnp.dot(built, own, preferred_element_type=jnp.float32), pl.ds(pl.multiple_of(core * width, LANES), width))
    put(
        jnp.dot(built, slab_rows(other_ref, 0, BLK), preferred_element_type=jnp.float32),
        pl.ds(pl.multiple_of((1 - core) * width, LANES), width),
    )


def gather_groups(groups, start):
    return jnp.concatenate([g[:, start : start + HALF] for g in groups], axis=1)


def sum_aux(in_ref, out_ref):
    basis = in_ref.shape[2]
    half = basis // LANES // 2

    def total(tile):
        cols = slice(tile * LANES, (tile + 1) * LANES)
        value = in_ref[0, :, cols].astype(jnp.float32)
        for k in range(1, in_ref.shape[0]):
            value = value + in_ref[k, :, cols].astype(jnp.float32)
        return [value[8 * g : 8 * g + 8] for g in range(4)]

    for tile in range(half):
        cores = [total(tile), total(tile + half)]
        for q in range(4):
            slot = (tile * 4 + q - TURN) % PLANES
            both = jnp.concatenate([gather_groups(groups, q * HALF) for groups in cores])
            out_ref[slot * PACK : (slot + 1) * PACK, :] = both.astype(out_ref.dtype)


def sum_planes(in_ref, out_ref):
    total = in_ref[:PACK, :].astype(jnp.float32)
    for z in range(1, PLANES):
        total = total + in_ref[z * PACK : (z + 1) * PACK, :].astype(jnp.float32)
    parts = [total[8 * core : 8 * core + 8, g * HALF : (g + 1) * HALF] for core in range(2) for g in range(4)]
    out_ref[...] = jnp.concatenate(parts, axis=0).T


def body(three_centre, density, pair_mask, density_mask):
    aux, height, basis = three_centre.shape
    width = basis // 2
    bf16, f32 = jnp.bfloat16, jnp.float32
    swap = [(0, 1), (1, 0)]
    planes = PLANES
    half = jax.ShapeDtypeStruct((aux, height, width), bf16)
    most = jax.ShapeDtypeStruct((aux - 1, height, width), bf16)
    last = jax.ShapeDtypeStruct((1, height, width), bf16)
    piece, keep, send, send_last = pl.pallas_call(
        prepare,
        out_shape=(jax.ShapeDtypeStruct((planes, PACK, LANES), bf16), half, most, last),
        in_specs=[pl.BlockSpec(memory_space=pltpu.HBM)] * 4,
        out_specs=(pl.BlockSpec(memory_space=pltpu.HBM), vmem(), vmem(), vmem()),
        scratch_shapes=[
            VMEM(three_centre.shape, bf16),
            VMEM((PACK, LANES), bf16),
            VMEM((planes, PACK, LANES), bf16),
            SMEM(pair_mask.shape, jnp.int32),
            SMEM(density_mask.shape, jnp.int32),
            pltpu.SemaphoreType.DMA((4 + aux,)),
        ],
        compiler_params=pltpu.CompilerParams(vmem_limit_bytes=40 << 20),
        name="prepare",
    )(*(pltpu.with_memory_space_constraint(a, pltpu.HBM) for a in (three_centre, density, pair_mask, density_mask)))
    late_first = [(i + FIRST) % PLANES for i in range(PLANES)]
    along_z = lax.all_to_all(piece, "z", 0, 0, axis_index_groups=[late_first], tiled=True)
    got = lax.all_gather(send, "core", axis=0, tiled=True)
    got_last = lax.all_gather(send_last, "core", axis=0, tiled=True)
    both = pl.pallas_call(
        join,
        out_shape=jax.ShapeDtypeStruct((2 * aux, height, width), bf16),
        in_specs=[vmem()] * 3,
        out_specs=vmem(),
        compiler_params=pltpu.CompilerParams(vmem_limit_bytes=32 << 20),
        name="join",
    )(keep, got, got_last)
    slabs = pl.pallas_call(
        pack,
        out_shape=jax.ShapeDtypeStruct((2 * aux, 2 * height, width), bf16),
        in_specs=[vmem()] * 2,
        out_specs=vmem(),
        compiler_params=pltpu.CompilerParams(vmem_limit_bytes=32 << 20),
        name="pack",
    )(both, along_z)
    from_corner = [[(i + SHIFT) % ROWS for i in range(ROWS)]]
    own = lax.all_to_all(slabs, ROW, 0, 0, axis_index_groups=from_corner, tiled=True)
    other = lax.ppermute(own, "core", swap)
    den_scratch = VMEM((planes, 2, PACK, basis), bf16)
    own_sum = pl.pallas_call(
        begin,
        out_shape=jax.ShapeDtypeStruct((width, basis), f32),
        in_specs=[vmem()],
        out_specs=vmem(),
        scratch_shapes=[den_scratch],
        compiler_params=pltpu.CompilerParams(vmem_limit_bytes=32 << 20),
        cost_estimate=pl.CostEstimate(flops=width * width * basis * 2, bytes_accessed=4 << 20, transcendentals=0),
        name="begin",
    )(own)
    partial = pl.pallas_call(
        contract,
        out_shape=jax.ShapeDtypeStruct((2 * aux, HALF, basis), bf16),
        in_specs=[vmem()] * 3,
        out_specs=vmem(),
        scratch_shapes=[den_scratch],
        compiler_params=pltpu.CompilerParams(vmem_limit_bytes=40 << 20),
        name="contract",
    )(own, other, own_sum)
    pieces = lax.all_to_all(partial, ROW, 0, 0, axis_index_groups=from_corner, tiled=True)
    packed = pl.pallas_call(
        sum_aux,
        out_shape=jax.ShapeDtypeStruct((PLANES * PACK, LANES), bf16),
        in_specs=[vmem()],
        out_specs=vmem(),
        compiler_params=pltpu.CompilerParams(vmem_limit_bytes=16 << 20),
        name="sum_aux",
    )(pieces)
    turned = [(i + TURN) % PLANES for i in range(PLANES)]
    pairs = [[2 * z + c for z in turned for c in range(2)]]
    arrived = lax.all_to_all(packed, COL, 0, 0, axis_index_groups=pairs, tiled=True)
    return pl.pallas_call(
        sum_planes,
        out_shape=jax.ShapeDtypeStruct((HALF, BLK), f32),
        in_specs=[vmem()],
        out_specs=vmem(),
        compiler_params=pltpu.CompilerParams(vmem_limit_bytes=16 << 20),
        name="sum_planes",
    )(arrived).T


def solution(mesh):
    fine = Mesh(mesh.devices.reshape(4, 4, 16, 2), AXES)
    return jax.shard_map(
        body,
        mesh=fine,
        in_specs=(P(COL, ROW, None), P(COL, None), P(), P()),
        out_specs=P(ROW, COL),
        check_vma=False,
    )
```
